512 devices in a mesh: wedge: 64 (over y, z_lo, core), filt: 8 (over x, z_hi).
Axes of the slice: x: 4, y: 4, z: 16 (z_hi: 2, z_lo: 8; z = z_hi * 8 + z_lo), core: 2. Of those that a mesh axis runs over, the one named last changes fastest.
Arguments:
- x_in: bfloat16 [256, 8, 2, 1024], P('filt', None, None, 'wedge'), may hold values from -6 to 6
- h_prev: bfloat16 [256, 8, 2, 1024], P('filt', None, None, 'wedge'), may hold values from -1.25 to 1.25
- reset: int32 [8], replicated, may hold values from 0 to 1, as said below
- w_gate: bfloat16 [2, 3, 3, 256, 2, 256], P(None, None, None, 'filt'), may hold values from -0.09375 to 0.09375
- gate_bias: float32 [2, 256], P(None, 'filt'), may hold values from -3 to 3
- w_cand: bfloat16 [2, 3, 3, 256, 256], P(None, None, None, 'filt'), may hold values from -0.15625 to 0.15625
- cand_bias: float32 [256], P('filt'), may hold values from -3 to 3
- cotangent: bfloat16 [256, 8, 2, 1024], P('filt', None, None, 'wedge'), may hold values from -6 to 6
Outputs:
- h_new: bfloat16 [256, 8, 2, 1024], P('filt', None, None, 'wedge')
- grad_x: bfloat16 [256, 8, 2, 1024], P('filt', None, None, 'wedge')
- grad_h: bfloat16 [256, 8, 2, 1024], P('filt', None, None, 'wedge')
- grad_w_gate: float32 [2, 3, 3, 256, 2, 256], P(None, None, None, 'filt')
- grad_gate_bias: float32 [2, 256], P(None, 'filt')
- grad_w_cand: float32 [2, 3, 3, 256, 256], P(None, None, None, 'filt')
- grad_cand_bias: float32 [256], P('filt')
The draws below stay inside these ranges and needn't reach their ends.
Inputs may be any that keep to these rules, and one draw needn't show every extreme that they name: `reset`: 1 marks a sample that starts a new forecast at this step; every draw has at least one sample with 1 and at least one with 0.
All inputs are finite; a program needn't handle non-finite values.
Results may differ from the reference program's by a relative error of at most 0.017.
Values may be sent and summed in bfloat16 or wider, within the bound.
A program may use at most 64 MiB of HBM per device.

```python
import jax
import jax.numpy as jnp
from jax import lax

C = 256
BATCH = 8
CIRCLES = 2
LON = 1024
N_FILT = 8


def draw_reset(key, part):
    key = jax.random.fold_in(key, 11)
    first_key, second_key = jax.random.split(key)
    order = jax.random.permutation(first_key, BATCH)
    count = jax.random.randint(second_key, (), 1, BATCH)
    return (order < count).astype(jnp.int32)


def block_levels(stream_key, shape, cuts, least, largest):
    def one(axis_at, parts):
        draws = jax.random.uniform(jax.random.fold_in(jax.random.fold_in(stream_key, 6), axis_at), (parts,), jnp.float32, least / len(cuts), largest / len(cuts))
        return jnp.repeat(jnp.exp(draws), shape[axis_at] // parts).reshape((-1,) + (1,) * (len(shape) - axis_at - 1))

    factor_of = one(*cuts[0])
    for cut in cuts[1:]:
        factor_of = factor_of * one(*cut)
    return factor_of


def normal_values(own_key, extent, spread, reach, shards=(), held_as=jnp.bfloat16):
    values = spread * jax.random.normal(own_key, extent, jnp.float32)
    if shards:
        values = values * block_levels(own_key, extent, shards, -0.22, 0.18)
    return jnp.clip(values, -reach, reach).astype(held_as)


def setup_inputs(seed: int = 0) -> dict:
    key_list = jax.random.split(jax.random.key(seed), 9)
    x_in = normal_values(key_list[0], (C, BATCH, CIRCLES, LON), 1.0, 6.0, ((0, 8), (3, 64)))
    h_prev = jnp.clip(jax.random.uniform(key_list[1], (C, BATCH, CIRCLES, LON), jnp.float32, -1.25, 1.25) * block_levels(key_list[1], (C, BATCH, CIRCLES, LON), ((0, 8), (3, 64)), -0.4, 0.0), -1.25, 1.25).astype(jnp.bfloat16)
    reset = draw_reset(jax.random.fold_in(key_list[8], 71), 0)
    w_gate = normal_values(key_list[3], (2, 3, 3, C, 2, C), (18 * C) ** -0.5, 0.09375, ((3, 8),))
    gate_bias = normal_values(key_list[4], (2, C), 0.8, 3.0, ((1, 8),), jnp.float32)
    w_cand = normal_values(key_list[5], (2, 3, 3, C, C), (6 * C) ** -0.5, 0.15625, ((3, 8),))
    cand_bias = normal_values(key_list[6], (C,), 0.8, 3.0, ((0, 8),), jnp.float32)
    cotangent = normal_values(key_list[7], (C, BATCH, CIRCLES, LON), 1.0, 6.0, ((0, 8), (3, 64)))
    return {"x_in": x_in, "h_prev": h_prev, "reset": reset, "w_gate": w_gate, "gate_bias": gate_bias, "w_cand": w_cand, "cand_bias": cand_bias, "cotangent": cotangent}


def circle_pad(field):
    return jnp.pad(field, ((0, 0), (0, 0), (1, 1), (0, 0)))

def wrap_pad(field):
    return jnp.concatenate([field[..., -1:], field, field[..., :1]], axis=3)

def tap_view(padded, row_step, col_step, circles, width):
    return padded[:, :, row_step:row_step + circles, col_step:col_step + width]

def blocked_conv(first, second, weights, circles, width):
    chans = first.shape[0]
    block = chans // N_FILT
    total = None
    for index in range(N_FILT):
        lower = index * block
        columns = []
        for field in (first, second):
            padded = circle_pad(field[lower:lower + block])
            for row_step in range(3):
                for col_step in range(3):
                    columns.append(tap_view(padded, row_step, col_step, circles, width).reshape(block, -1))
        columns = jnp.concatenate(columns, axis=0)
        matrix = weights[:, :, :, lower:lower + block].reshape(18 * block, -1)
        partial_sum = jnp.dot(matrix.T, columns, preferred_element_type=jnp.float32)
        partial_sum = lax.optimization_barrier(partial_sum.astype(jnp.bfloat16)).astype(jnp.float32)
        total = partial_sum if total is None else total + partial_sum
    return total

def adjoint(grad, weights, circles, width):
    chans = weights.shape[3]
    flat_w = weights.reshape(2, 3, 3, chans, -1)
    padded = circle_pad(wrap_pad(grad))
    outer = grad.shape[0]
    first = jnp.zeros((chans, grad[0].size), jnp.float32)
    second = jnp.zeros((chans, grad[0].size), jnp.float32)
    for row_step in range(3):
        for col_step in range(3):
            view = tap_view(padded, 2 - row_step, 2 - col_step, circles, width).reshape(outer, -1)
            first = first + jnp.dot(flat_w[0, row_step, col_step], view, preferred_element_type=jnp.float32)
            second = second + jnp.dot(flat_w[1, row_step, col_step], view, preferred_element_type=jnp.float32)
    return (first, second)

def weight_grad(first, second, grad_flat, circles, width):
    pieces = []
    for field in (first, second):
        padded = circle_pad(field)
        for row_step in range(3):
            for col_step in range(3):
                view = tap_view(padded, row_step, col_step, circles, width).reshape(field.shape[0], -1)
                pieces.append(lax.dot_general(view, grad_flat, (((1,), (1,)), ((), ())), preferred_element_type=jnp.float32))
    stacked = jnp.stack(pieces)
    return stacked.reshape((2, 3, 3) + stacked.shape[1:])

def reference(x_in, h_prev, reset, w_gate, gate_bias, w_cand, cand_bias, cotangent):
    chans, batch, circles, width = x_in.shape
    shape = x_in.shape
    keep = (1 - reset).astype(jnp.bfloat16)[None, :, None, None]
    start_h = h_prev * keep
    x_wide = wrap_pad(x_in)
    h_wide = wrap_pad(start_h)
    gate_pre = blocked_conv(x_wide, h_wide, w_gate, circles, width).reshape(2, chans, -1) + gate_bias[:, :, None]
    update = jax.nn.sigmoid(gate_pre[0])
    reset_gate = jax.nn.sigmoid(gate_pre[1])
    h_flat = start_h.reshape(chans, -1).astype(jnp.float32)
    gated = (reset_gate * h_flat).astype(jnp.bfloat16).reshape(shape)
    gated_wide = wrap_pad(gated)
    cand_pre = blocked_conv(x_wide, gated_wide, w_cand, circles, width) + cand_bias[:, None]
    fresh = jnp.tanh(cand_pre)
    h_new = ((1.0 - update) * h_flat + update * fresh).astype(jnp.bfloat16).reshape(shape)
    grad_out = cotangent.reshape(chans, -1).astype(jnp.float32)
    cand_grad = (grad_out * update * (1.0 - fresh * fresh)).astype(jnp.bfloat16)
    back_x, gated_grad = adjoint(cand_grad.reshape(shape), w_cand, circles, width)
    update_term = grad_out * (fresh - h_flat) * update * (1.0 - update)
    reset_term = gated_grad * h_flat * reset_gate * (1.0 - reset_gate)
    gate_grad = jnp.stack([update_term, reset_term]).astype(jnp.bfloat16)
    up_x, up_h = adjoint(gate_grad.reshape(2 * chans, batch, circles, width), w_gate, circles, width)
    grad_x = (back_x + up_x).astype(jnp.bfloat16).reshape(shape)
    keep_f = (1 - reset).astype(jnp.float32)[None, :, None, None]
    grad_h = ((grad_out * (1.0 - update) + gated_grad * reset_gate + up_h).reshape(shape) * keep_f).astype(jnp.bfloat16)
    grad_w_gate = weight_grad(x_wide, h_wide, gate_grad.reshape(2 * chans, -1), circles, width).reshape(2, 3, 3, chans, 2, chans)
    grad_w_cand = weight_grad(x_wide, gated_wide, cand_grad, circles, width)
    grad_gate_bias = lax.optimization_barrier(jnp.sum(gate_grad.astype(jnp.float32), axis=2))
    grad_cand_bias = lax.optimization_barrier(jnp.sum(cand_grad.astype(jnp.float32), axis=1))
    return (h_new, grad_x, grad_h, grad_w_gate, grad_gate_bias, grad_w_cand, grad_cand_bias)
```

```python
import functools

import numpy as np
import jax
import jax.numpy as jnp
from jax import lax
from jax.experimental import pallas as pl
from jax.experimental.pallas import tpu as pltpu
from jax.sharding import PartitionSpec as P

XN, ZH, YN, ZL, CN = 4, 2, 4, 8, 2
WEDGES = YN * ZL * CN
MESH = pl.DeviceIdType.MESH
BF = jnp.bfloat16
F32 = jnp.float32
NT = (((1,), (1,)), ((), ()))


def block_transpose(first, second, third):
    size = first * second * third
    order = np.arange(size).reshape(first, second, third).transpose(1, 0, 2).reshape(-1)
    matrix = np.zeros((size, size), np.float32)
    matrix[order, np.arange(size)] = 1.0
    return matrix


def two_step():
    order = np.arange(256).reshape(4, 2, 32).transpose(1, 0, 2).reshape(-1)
    matrix = np.zeros((256, 256), np.float32)
    matrix[order, np.arange(256)] = 1.0
    return matrix


def roll(v, shift):
    return pltpu.roll(v, shift, 1)


def lanes(shape):
    return lax.broadcasted_iota(jnp.int32, shape, 1)


def slot_a(shape):
    return lanes(shape) % 64 < 32


def swap(v):
    return jnp.where(slot_a(v.shape), roll(v, 96), roll(v, 32))


def dot(a, b):
    return jnp.dot(a, b, preferred_element_type=F32)


def dot_nt(a, b):
    return lax.dot_general(a, b, NT, preferred_element_type=F32)


def kernel(
    f_ref, wg_ref, wc_ref, gb_ref, cb_ref, q4_ref, q2_ref, q5_ref,
    field_ref, wgg_ref, wgc_ref, bias_ref,
    halo_l, halo_r, uf, vf, cotf, wgf, wcf, wback, wr,
    gsend, grecv, gzs, gzr, csend, crecv, czs, czr, g1, rzs, rzr, g2, ut, vt,
    blob1, blob2, r1, r2, zs, zr, zf, fin, bs, br, bs2, br2,
    s_halo, r_halo, s_g, r_g, s_c, r_c, s_a, r_a, s_b, r_b, s_w1, r_w1, s_w2, r_w2,
    s_zs, r_zs, s_zf, r_zf, s_f, r_f, s_bi, r_bi,
):
    w = lax.axis_index("wedge")
    f = lax.axis_index("filt")
    x, zh = f // ZH, f % ZH
    core, zl, yy = w % CN, (w // CN) % ZL, w // (CN * ZL)
    m = yy * CN + core

    def xpeer(d):
        return (w, ((x + d) % XN) * ZH + zh)

    zpartner = (w, x * ZH + (1 - zh))
    right = ((w + 1) % WEDGES, f)
    left = ((w + WEDGES - 1) % WEDGES, f)

    def mpeer(d):
        t = (m + d) % 8
        return ((t // CN) * ZL + zl) * CN + t % CN, f

    def lpeer(d):
        return (yy * ZL + (zl + d) % ZL) * CN + core, f

    peers = [left, right, zpartner] + [xpeer(d) for d in (1, 2, 3)]
    peers += [mpeer(d) for d in range(1, 8)] + [lpeer(d) for d in range(1, 8)]
    barrier = pltpu.get_barrier_semaphore()
    for peer in peers:
        pl.semaphore_signal(barrier, inc=1, device_id=peer, device_id_type=MESH)
    pl.semaphore_wait(barrier, len(peers))

    sends = []

    def push(src, dst, send_sem, recv_sem, peer):
        copy = pltpu.make_async_remote_copy(
            src_ref=src, dst_ref=dst, send_sem=send_sem, recv_sem=recv_sem,
            device_id=peer, device_id_type=MESH,
        )
        copy.start()
        sends.append(copy)
        return copy

    hr = push(f_ref.at[pl.ds(96, 32), :], halo_l, s_halo.at[0], r_halo.at[0], right)
    hl = push(f_ref.at[pl.ds(0, 32), :], halo_r, s_halo.at[1], r_halo.at[1], left)

    def nat(ref, a, e, lo, hi):
        return jnp.concatenate(
            [ref[((s * 3 + a) * 3 + e) * 32:((s * 3 + a) * 3 + e) * 32 + 32, lo:hi] for s in range(2)],
            axis=0,
        )

    blocks = [(e, ip) for e in range(3) for ip in range(2)]
    q4, q5 = q4_ref[...], q5_ref[...]
    for fh in range(2):
        lo = fh * 128
        lhs = jnp.concatenate(
            [
                jnp.concatenate(
                    [nat(wg_ref, a, e, g * 256 + lo, g * 256 + lo + 128) for a in (ip + 1, ip) for g in range(2)],
                    axis=1,
                )
                for e, ip in blocks
            ],
            axis=0,
        )
        out = dot(lhs, q4).astype(BF)
        wgf[2 * fh] = out[:, :256]
        wgf[2 * fh + 1] = out[:, 256:]
        masked = jnp.where(slot_a((384, 512)), out, jnp.zeros_like(out))
        zero = jnp.zeros((64, 128), BF)
        lhs = jnp.concatenate(
            [
                jnp.concatenate(
                    [zero, nat(wc_ref, ip + 1, e, lo, lo + 128), zero, nat(wc_ref, ip, e, lo, lo + 128)], axis=1
                )
                for e, ip in blocks
            ],
            axis=0,
        )
        out = dot(lhs, q4).astype(BF)
        for xl in range(2):
            cols = slice(xl * 256, xl * 256 + 256)
            for e in range(3):
                wback[2 * fh + xl, e * 256:e * 256 + 128, :] = out[e * 128:e * 128 + 128, cols]
                wback[2 * fh + xl, e * 256 + 128:e * 256 + 256, :] = masked[e * 128:e * 128 + 128, cols]
    for ref, lo, place in ((wc_ref, 0, "c"), (wg_ref, 256, "r")):
        lhs = jnp.concatenate(
            [
                jnp.concatenate([nat(ref, a, e, lo, lo + 256) for a in (ip + 1, ip)], axis=1)
                for e, ip in blocks
            ],
            axis=0,
        )
        out = dot_nt(lhs, q5).astype(BF)
        if place == "c":
            for t in range(4):
                wcf[t] = out[:, t * 128:t * 128 + 128]
        else:
            wr[...] = out

    uf[32:160, :] = f_ref[:, :128].astype(F32)
    cotf[16:144, :] = f_ref[:, 128:].astype(F32)
    hr.wait_recv()
    hl.wait_recv()
    uf[0:32, :] = halo_l[:, :128].astype(F32)
    uf[160:192, :] = halo_r[:, :128].astype(F32)
    cotf[0:16, :] = halo_l[:, 128:].astype(F32)[16:32]
    cotf[144:160, :] = halo_r[:, 128:].astype(F32)[0:16]

    lhs = jnp.concatenate([uf[e * 8:e * 8 + 176, :].astype(BF) for e in range(3)], axis=1)
    arriving = []
    for k, d in enumerate((2, 1, 3, 0)):
        t = (x + d) % XN
        part = dot(lhs, wgf[t]).astype(BF)
        gsend[t] = part
        if d:
            arriving.append(push(gsend.at[t], grecv.at[d - 1], s_g.at[d - 1], r_g.at[d - 1], xpeer(d)))
    for e in range(3):
        ut[e * 128:e * 128 + 128, :] = uf[(e + 3) * 8:(e + 3) * 8 + 128, :].T.astype(BF)
    total = gsend[x].astype(F32)
    for k, d in enumerate((2, 1, 3)):
        arriving[k].wait_recv()
        total = total + grecv[d - 1].astype(F32)
    first_z = zh == 0
    gzs[...] = jnp.where(first_z, total[:, 128:], total[:, :128]).astype(BF)
    gz = push(gzs, gzr, s_g.at[3], r_g.at[3], zpartner)
    mine = jnp.where(first_z, total[:, :128], total[:, 128:]) + gb_ref[0:1, :]
    gz.wait_recv()
    sg = jax.nn.sigmoid(mine + gzr[...].astype(F32))
    u_near = uf[8:184, :]
    vf[...] = jnp.where(slot_a((176, 128)), u_near, (sg * u_near).astype(BF).astype(F32))

    lhs = jnp.concatenate([vf[e * 8:e * 8 + 160, :].astype(BF) for e in range(3)], axis=1)
    arriving = []
    for d in (2, 1, 3, 0):
        t = (x + d) % XN
        part = dot(lhs, wcf[t]).astype(BF)
        csend[t] = part
        if d:
            arriving.append(push(csend.at[t], crecv.at[d - 1], s_c.at[d - 1], r_c.at[d - 1], xpeer(d)))
    for e in range(3):
        vt[e * 128:e * 128 + 128, :] = vf[(e + 2) * 8:(e + 2) * 8 + 128, :].T.astype(BF)
    total = csend[x].astype(F32)
    for k, d in enumerate((2, 1, 3)):
        arriving[k].wait_recv()
        total = total + crecv[d - 1].astype(F32)
    half_slot = (lanes((80, 128)) // 32) % 2
    czs[...] = jnp.where(half_slot != zh, total[:80], swap(total[80:])).astype(BF)
    cz = push(czs, czr, s_c.at[3], r_c.at[3], zpartner)
    cz.wait_recv()
    got = czr[...].astype(F32)
    total = total + jnp.concatenate([got, swap(got)], axis=0)
    cand = jnp.where(first_z, total, swap(total)) + cb_ref[0:1, :]
    fresh = jnp.tanh(cand)
    u = sg[8:168]
    h = swap(uf[16:176, :])
    cot = cotf[...]
    hn = (1.0 - u) * h + u * fresh
    cg = cot * u * (1.0 - fresh * fresh)
    upd = cot * (fresh - h) * u * (1.0 - u)
    direct = cot * (1.0 - u)
    msg = jnp.where(slot_a((160, 128)), upd, swap(cg)).astype(BF)
    g1[f] = msg
    fp = x * ZH + (1 - zh)
    az = push(g1.at[f], g1.at[f], s_a.at[0], r_a.at[0], zpartner)
    own = [push(g1.at[f], g1.at[f], s_a.at[d], r_a.at[d], xpeer(d)) for d in (2, 1, 3)]
    field_ref[:, :128] = hn[16:144].astype(BF)
    sum1 = jnp.sum(msg[16:144].astype(F32), axis=0, keepdims=True)
    az.wait_recv()
    forwarded = [push(g1.at[fp], g1.at[fp], s_a.at[3 + d], r_a.at[3 + d], xpeer(d)) for d in (2, 1, 3)]
    for copy in own + forwarded:
        copy.wait_recv()

    back = None
    for t in range(4):
        part = dot_nt(jnp.concatenate([g1[2 * t], g1[2 * t + 1]], axis=1), wback[t])
        back = part if back is None else back + part
    first = None
    second = None
    for e in range(3):
        a = back[(2 - e) * 8:(2 - e) * 8 + 144, e * 256:e * 256 + 128]
        b = back[(3 - e) * 8:(3 - e) * 8 + 128, e * 256 + 128:e * 256 + 256]
        first = a if first is None else first + a
        second = b if second is None else second + b
    r_near = sg[16:160]
    rt = (first * uf[24:168, :] * r_near * (1.0 - r_near)).astype(BF).astype(F32)
    sum2 = jnp.sum(rt[8:136], axis=0, keepdims=True)
    edge = jnp.zeros((8, 128), F32)
    rt = jnp.concatenate([edge, rt, edge], axis=0)
    rz = jnp.where(first_z, swap(rt), rt)
    rzs[...] = jnp.where(half_slot == zh, rz[:80], swap(rz[80:])).astype(BF)
    bz = push(rzs, rzr, s_b.at[0], r_b.at[0], zpartner)

    low = lanes((64, 128)) < 64
    upper = slot_a((128, 256))

    def slabs(res):
        t0, t1 = res[:, :128], res[:, 128:]
        return (
            jnp.where(low, t0[64:], t0[:64]),
            jnp.where(low, t1[64:], t1[:64]),
            jnp.where(low, t0[:64] + roll(t0[64:], 64), t1[64:] + roll(t1[:64], 64)),
        )

    for t in range(4):
        rhs = jnp.concatenate([g1[2 * t, 16:144, :], g1[2 * t + 1, 16:144, :]], axis=1)
        for e in range(3):
            rows = slice(e * 128, e * 128 + 128)
            res = jnp.where(upper, dot(ut[rows, :], rhs), dot(vt[rows, :], rhs))
            for k, slab in enumerate(slabs(res)):
                n = e * 12 + t * 3 + k
                blob1[n * 64:n * 64 + 64, :] = slab.astype(BF)
    w1 = []
    for d in range(1, 8):
        t = (m + d) % 8
        w1.append(
            push(
                blob1.at[pl.ds(pl.multiple_of(t * 288, 32), 288), :], r1.at[d - 1], s_w1.at[d - 1], r_w1.at[d - 1],
                mpeer(d),
            )
        )

    bz.wait_recv()
    got = rzr[...].astype(F32)
    full_slot = (lanes((160, 128)) // 32) % 2
    g2[x] = jnp.where(full_slot == zh, rz, jnp.concatenate([got, swap(got)], axis=0)).astype(BF)
    bx = [push(g2.at[x], g2.at[x], s_b.at[d], r_b.at[d], xpeer(d)) for d in (2, 1, 3)]
    row = lax.broadcasted_iota(jnp.int32, (8, 128), 0)
    bs[...] = jnp.where(row == 0, sum1, jnp.where(row == 1, sum2, 0.0))
    bias1 = [push(bs, br.at[d - 1], s_bi.at[d - 1], r_bi.at[d - 1], mpeer(d)) for d in range(1, 8)]
    for copy in bx:
        copy.wait_recv()

    for q in range(2):
        rhs = jnp.concatenate([g2[2 * q, 16:144, :], g2[2 * q + 1, 16:144, :]], axis=1)
        for e in range(3):
            res = dot(ut[e * 128:e * 128 + 128, :], rhs)
            for k, slab in enumerate(slabs(res)):
                n = e * 6 + q * 3 + k
                blob2[n * 64:n * 64 + 64, :] = slab.astype(BF)
    w2 = []
    for d in range(1, 8):
        t = (m + d) % 8
        w2.append(
            push(
                blob2.at[pl.ds(pl.multiple_of(t * 144, 16), 144), :], r2.at[d - 1], s_w2.at[d - 1], r_w2.at[d - 1],
                mpeer(d),
            )
        )
    back = dot_nt(jnp.concatenate([g2[t] for t in range(4)], axis=1), wr[...])
    for e in range(3):
        second = second + back[(3 - e) * 8:(3 - e) * 8 + 128, e * 128:e * 128 + 128]
    center = first[8:136]
    mixed = jnp.where(slot_a((128, 128)), center, swap(direct[16:144]) + center * sg[24:152])
    field_ref[:, 128:] = (mixed + second).astype(BF)

    t1 = blob1[pl.ds(pl.multiple_of(m * 288, 32), 288), :].astype(F32)
    for d in range(1, 8):
        w1[d - 1].wait_recv()
        t1 = t1 + r1[d - 1].astype(F32)
    for p in range(4):
        zs[p] = t1[p * 64:p * 64 + 64].astype(BF)
    b1 = bs[...]
    for d in range(1, 8):
        bias1[d - 1].wait_recv()
        b1 = b1 + br[d - 1]
    bs2[...] = b1
    bias2 = [push(bs2, br2.at[d - 1], s_bi.at[6 + d], r_bi.at[6 + d], lpeer(d)) for d in range(1, 8)]
    t2 = blob2[pl.ds(pl.multiple_of(m * 144, 16), 144), :].astype(F32)
    for d in range(1, 8):
        w2[d - 1].wait_recv()
        t2 = t2 + r2[d - 1].astype(F32)
    zs[4] = jnp.concatenate([t1[256:288], t2[:32]], axis=0).astype(BF)
    zs[5] = t2[32:96].astype(BF)
    zs[6] = jnp.concatenate([t2[96:144], jnp.zeros((16, 128), F32)], axis=0).astype(BF)
    zs[7] = jnp.zeros((64, 128), BF)
    zc = []
    for d in range(1, 8):
        t = (zl + d) % ZL
        zc.append(push(zs.at[t], zr.at[d - 1], s_zs.at[d - 1], r_zs.at[d - 1], lpeer(d)))
    total = zs[zl].astype(F32)
    for d in range(1, 8):
        zc[d - 1].wait_recv()
        total = total + zr[d - 1].astype(F32)
    zf[zl] = total.astype(BF)
    zc = [push(zf.at[zl], zf.at[zl], s_zf.at[d - 1], r_zf.at[d - 1], lpeer(d)) for d in range(1, 8)]
    b2 = bs2[...]
    for d in range(1, 8):
        bias2[d - 1].wait_recv()
        b2 = b2 + br2[d - 1]
    bias_ref[...] = b2
    for copy in zc:
        copy.wait_recv()
    for p in range(6):
        fin[m, p * 64:p * 64 + 64, :] = zf[p]
    fin[m, 384:432, :] = zf[6, 0:48, :]
    fc = [push(fin.at[m], fin.at[m], s_f.at[d - 1], r_f.at[d - 1], mpeer(d)) for d in range(1, 8)]
    for copy in fc:
        copy.wait_recv()

    def slab1(n):
        out = []
        for r in range(n * 64, n * 64 + 64, 32):
            out.append(fin[r // 288, r % 288:r % 288 + 32, :])
        return jnp.concatenate(out, axis=0)

    def slab2(n):
        out = []
        for r in range(n * 64, n * 64 + 64, 16):
            at = 288 + r % 144
            out.append(fin[r // 144, at:at + 16, :])
        return jnp.concatenate(out, axis=0)

    def put(ref, a, e, lo, value):
        for s in range(2):
            at = ((s * 3 + a) * 3 + e) * 32
            ref[at:at + 32, lo:lo + value.shape[1]] = value[s * 32:s * 32 + 32]

    for fh in range(2):
        outer = jnp.concatenate(
            [
                jnp.concatenate([slab1(e * 12 + (2 * fh + xl) * 3 + k) for xl in range(2) for k in range(2)], axis=1)
                for e in range(3)
            ],
            axis=0,
        )
        outer = dot(outer, q4)
        inner = jnp.concatenate(
            [
                jnp.concatenate([slab1(e * 12 + (2 * fh + xl) * 3 + 2) for xl in range(2)], axis=1)
                for e in range(3)
            ],
            axis=0,
        )
        inner = dot(inner, q2_ref[...])
        for e in range(3):
            rows = slice(e * 64, e * 64 + 64)
            for k, ref in enumerate((wgg_ref, wgc_ref)):
                put(ref, 2, e, fh * 128, outer[rows, k * 128:k * 128 + 128])
                put(ref, 0, e, fh * 128, outer[rows, 256 + k * 128:384 + k * 128])
                put(ref, 1, e, fh * 128, inner[rows, k * 128:k * 128 + 128])
    outer = jnp.concatenate(
        [
            jnp.concatenate([slab2(e * 6 + q * 3 + k) for q in range(2) for k in range(2)], axis=1)
            for e in range(3)
        ],
        axis=0,
    )
    outer = dot(outer, q5)
    for e in range(3):
        rows = slice(e * 64, e * 64 + 64)
        put(wgg_ref, 2, e, 256, outer[rows, :256])
        put(wgg_ref, 0, e, 256, outer[rows, 256:])
        inner = jnp.concatenate([slab2(e * 6 + q * 3 + 2) for q in range(2)], axis=1)
        put(wgg_ref, 1, e, 256, inner.astype(F32))
    for copy in sends:
        copy.wait_send()


def step_kernel(fields, wg, wc, gb, cb):
    vm = pltpu.VMEM
    dma = pltpu.SemaphoreType.DMA
    scratch = [
        vm((32, 256), BF), vm((32, 256), BF), vm((192, 128), F32), vm((176, 128), F32), vm((160, 128), F32),
        vm((4, 384, 256), BF), vm((4, 384, 128), BF), vm((4, 768, 256), BF), vm((384, 512), BF),
        vm((4, 176, 256), BF), vm((3, 176, 256), BF), vm((176, 128), BF), vm((176, 128), BF),
        vm((4, 160, 128), BF), vm((3, 160, 128), BF), vm((80, 128), BF), vm((80, 128), BF),
        vm((8, 160, 128), BF), vm((80, 128), BF), vm((80, 128), BF), vm((4, 160, 128), BF),
        vm((384, 128), BF), vm((384, 128), BF),
        vm((2304, 128), BF), vm((1152, 128), BF), vm((7, 288, 128), BF), vm((7, 144, 128), BF),
        vm((8, 64, 128), BF), vm((7, 64, 128), BF), vm((8, 64, 128), BF), vm((8, 432, 128), BF),
        vm((8, 128), F32), vm((7, 8, 128), F32), vm((8, 128), F32), vm((7, 8, 128), F32),
    ]
    for count in (2, 4, 4, 7, 4, 7, 7, 7, 7, 7, 14):
        scratch += [dma((count,)), dma((count,))]
    q4 = jnp.asarray(block_transpose(4, 4, 32), BF)
    q2 = jnp.asarray(two_step(), BF)
    q5 = jnp.asarray(block_transpose(4, 2, 64), BF)
    return pl.pallas_call(
        kernel,
        out_shape=(
            jax.ShapeDtypeStruct((128, 256), BF),
            jax.ShapeDtypeStruct((576, 512), F32),
            jax.ShapeDtypeStruct((576, 256), F32),
            jax.ShapeDtypeStruct((8, 128), F32),
        ),
        in_specs=[pl.BlockSpec(memory_space=pltpu.VMEM)] * 8,
        out_specs=[pl.BlockSpec(memory_space=pltpu.VMEM)] * 4,
        scratch_shapes=scratch,
        compiler_params=pltpu.CompilerParams(
            collective_id=0, has_side_effects=True, vmem_limit_bytes=48 * 1024 * 1024
        ),
        cost_estimate=pl.CostEstimate(flops=1_000_000_000, bytes_accessed=8_000_000, transcendentals=100_000),
    )(fields, wg, wc, gb, cb, q4, q2, q5)


def per_device(x_in, h_prev, reset, w_gate, gate_bias, w_cand, cand_bias, cotangent):
    chans, batch, circles, width = x_in.shape
    keep = (1 - reset).astype(BF)[None, :, None, None]
    start_h = h_prev * keep
    parts = jnp.stack([x_in, start_h, cotangent, jnp.zeros_like(cotangent)])
    parts = parts.reshape(2, 2, chans, batch, circles, width).transpose(5, 3, 0, 4, 1, 2)
    fields = parts.reshape(width * batch, 256)
    gb = jnp.broadcast_to(gate_bias.reshape(1, 1, 64), (8, 2, 64)).reshape(8, 128)
    cb = jnp.broadcast_to(cand_bias.reshape(1, 1, 32), (8, 4, 32)).reshape(8, 128)
    field, wgg, wgc, bias = step_kernel(
        fields, w_gate.reshape(576, 512), w_cand.reshape(576, 256), gb, cb
    )
    field = field.reshape(width, batch, 2, circles, 2, chans)
    back = lambda v: v.transpose(3, 1, 2, 0)
    h_new = back(field[:, :, 0, :, 0])
    grad_x = back(field[:, :, 1, :, 0])
    grad_h = back(field[:, :, 1, :, 1]) * keep
    sums = bias.reshape(8, 2, 2, chans).sum(axis=1)
    gb_grad = jnp.stack([sums[0, 0], sums[1, 1]])
    return (
        h_new, grad_x, grad_h, wgg.reshape(w_gate.shape), gb_grad, wgc.reshape(w_cand.shape), sums[0, 1],
    )


def solution(mesh):
    field = P("filt", None, None, "wedge")
    in_specs = (
        field, field, P(), P(None, None, None, "filt", None, None), P(None, "filt"),
        P(None, None, None, "filt", None), P("filt"), field,
    )
    out_specs = (
        field, field, field, P(None, None, None, "filt", None, None), P(None, "filt"),
        P(None, None, None, "filt", None), P("filt"),
    )
    return jax.shard_map(per_device, mesh=mesh, in_specs=in_specs, out_specs=out_specs, check_vma=False)
```

```python
import numpy as np
import jax
import jax.numpy as jnp
from jax import lax
from jax.experimental import pallas as pl
from jax.experimental.pallas import tpu as pltpu
from jax.sharding import PartitionSpec as P

XN, ZH, YN, ZL, CN = 4, 2, 4, 8, 2
WEDGES = YN * ZL * CN
COPIES = 104
MESH = pl.DeviceIdType.MESH
BF = jnp.bfloat16
F32 = jnp.float32
NT = (((1,), (1,)), ((), ()))


def block_transpose(first, second, third):
    size = first * second * third
    order = np.arange(size).reshape(first, second, third).transpose(1, 0, 2).reshape(-1)
    matrix = np.zeros((size, size), np.float32)
    matrix[order, np.arange(size)] = 1.0
    return matrix


def row_order():
    order = np.arange(128).reshape(8, 16).T.reshape(-1)
    matrix = np.zeros((128, 128), np.float32)
    matrix[np.arange(128), order] = 1.0
    return matrix


def roll(v, shift):
    return pltpu.roll(v, shift, 1)


def slot_a(shape):
    return lax.broadcasted_iota(jnp.int32, shape, 1) % 64 < 32


def swap(v):
    return jnp.where(slot_a(v.shape), roll(v, 96), roll(v, 32))


def dot(a, b):
    return jnp.dot(a, b, preferred_element_type=F32)


def dot_nt(a, b):
    return lax.dot_general(a, b, NT, preferred_element_type=F32)


def tiles(ref):
    return jnp.concatenate([ref[t] for t in range(4)], axis=1)


def taps(ref, start, rows):
    return jnp.concatenate([ref[start + e * 8:start + e * 8 + rows, :].astype(BF) for e in range(3)], axis=1)


def shifted(v, start, rows):
    out = None
    for e in range(3):
        part = v[start + (2 - e) * 8:start + (2 - e) * 8 + rows, e * 128:e * 128 + 128]
        out = part if out is None else out + part
    return out


def kernel(
    reset_ref, x_ref, h_ref, ct_ref, wg_ref, wc_ref, gb_ref, cb_ref, q5_ref, pm_ref,
    field_ref, fin_a, fin_r, bias_ref,
    f_ref, halo_l, halo_r, uf, near_l, near_r, far, hp, cp, wch, w_upd, w_res, w_cx, w_ch,
    bz_s, bz_r, gs_r, gr_r, gs_u, gr_u, zs_r, zr_r, zs_u, zr_u, gpf, cs, cr,
    g1c, g1u, g2, ut, vt, blob_a, blob_r, core_a, mid_a, y_a, m_r,
    zs_a, zq_a, zf_a, zs_b, zq_b, zf_b, bs, br, bs2, br2,
    send_sems, recv_sems,
):
    w = lax.axis_index("wedge")
    f = lax.axis_index("filt")
    x, zh = f // ZH, f % ZH
    core, zl, yy = w % CN, (w // CN) % ZL, w // (CN * ZL)
    m = yy * CN + core
    first_z = zh == 0
    fp = x * ZH + (1 - zh)
    after, before = (w + 1) % WEDGES, (w + WEDGES - 1) % WEDGES

    def xpeer(d):
        return (w, ((x + d) % XN) * ZH + zh)

    def at_y(t, c):
        return (t * ZL + zl) * CN + c, f

    def mpeer(d):
        t = (m + d) % 8
        return at_y(t // CN, t % CN)

    def ypeer(d):
        return at_y((yy + d) % YN, core)

    def lpeer(d):
        return (yy * ZL + (zl + d) % ZL) * CN + core, f

    partner = (w, fp)
    other_core = at_y(yy, 1 - core)
    peers = [(after, f), (before, f), (after, fp), (before, fp), partner] + [xpeer(d) for d in (1, 2, 3)]
    peers += [mpeer(d) for d in range(1, 8)] + [lpeer(d) for d in range(1, 8)]
    barrier = pltpu.get_barrier_semaphore()
    for peer in peers:
        pl.semaphore_signal(barrier, inc=1, device_id=peer, device_id_type=MESH)

    def own_a(v):
        return jnp.where(first_z, v, swap(v))

    def own_b(v):
        return jnp.where(first_z, swap(v), v)

    order = pm_ref[...]
    kept = jnp.concatenate(
        [h_ref[b:b + 1].astype(F32) * (1 - reset_ref[b]).astype(F32) for b in range(8)], axis=0
    )
    near, wide = [], []
    for i in range(2):
        hidden = kept[:, i].reshape(128, 32)
        near += [x_ref[:, i].reshape(128, 32).astype(F32), hidden]
        wide += [ct_ref[:, i].reshape(128, 32).astype(F32), hidden]
    own_u = dot(order, jnp.concatenate(near, axis=1).astype(BF))
    own_c = dot(order, jnp.concatenate(wide, axis=1).astype(BF))
    f_ref[:, :128] = own_u.astype(BF)
    f_ref[:, 128:] = own_c.astype(BF)
    uf[32:160, :] = own_u
    row = lax.broadcasted_iota(jnp.int32, (8, 128), 0)
    bias_rows = [jnp.concatenate([v] * 4, axis=1) for v in (gb_ref[0:1, :], gb_ref[1:2, :], cb_ref[...])]
    bias_rows = jnp.where(row == 0, bias_rows[0], jnp.where(row == 1, bias_rows[1], bias_rows[2]))
    bz_s[...] = jnp.where(slot_a((8, 128)) == first_z, bias_rows, 0.0)
    pl.semaphore_wait(barrier, len(peers))

    sends = []

    def push(src, dst, peer):
        at = len(sends)
        copy = pltpu.make_async_remote_copy(
            src_ref=src, dst_ref=dst, send_sem=send_sems.at[at], recv_sem=recv_sems.at[at],
            device_id=peer, device_id_type=MESH,
        )
        copy.start()
        sends.append(copy)
        return copy

    def landed(copies):
        for copy in copies:
            copy.wait_recv()

    right, left = pl.ds(96, 32), pl.ds(0, 32)
    second = pl.ds(128, 128)
    halo = [
        push(f_ref.at[right, :], halo_l, (after, f)),
        push(f_ref.at[left, :], halo_r, (before, f)),
    ]
    pair = [
        push(f_ref.at[right, second], near_l, (after, fp)),
        push(f_ref.at[left, second], near_r, (before, fp)),
        push(f_ref.at[:, second], far, partner),
        push(bz_s, bz_r, partner),
    ]
    pair_w = push(wc_ref.at[pl.ds(288, 288), :], wch.at[zh], partner)
    wch[zh] = wc_ref[288:576, :]
    q5 = q5_ref[...]

    def arrange(nat, out_ref):
        lhs = jnp.concatenate(
            [
                jnp.concatenate([nat(a, e) for a in (ip + 1, ip)], axis=1)
                for e in range(3)
                for ip in range(2)
            ],
            axis=0,
        )
        out = dot_nt(lhs, q5).astype(BF)
        for t in range(4):
            out_ref[t] = out[:, t * 128:t * 128 + 128]

    def both(ref, lo):
        def nat(a, e):
            rows = [((s * 3 + a) * 3 + e) * 32 for s in range(2)]
            return jnp.concatenate([ref[r:r + 32, lo:lo + 256] for r in rows], axis=0)

        return nat

    def input_only(a, e):
        at = (a * 3 + e) * 32
        return jnp.concatenate([wc_ref[at:at + 32, :], jnp.zeros((32, 256), BF)], axis=0)

    def pair_hidden(a, e):
        at = (a * 3 + e) * 32
        return jnp.concatenate([wch[0, at:at + 32, :], wch[1, at:at + 32, :]], axis=0)

    arrange(both(wg_ref, 256), w_res)
    arrange(both(wg_ref, 0), w_upd)
    arrange(input_only, w_cx)
    landed(halo)
    uf[0:32, :] = halo_l[:, :128].astype(F32)
    uf[160:192, :] = halo_r[:, :128].astype(F32)

    lhs = taps(uf, 0, 176)
    res = []
    for d in (2, 1, 3, 0):
        t = (x + d) % XN
        gs_r[t] = dot(lhs, w_res[t]).astype(BF)
        if d:
            res.append(push(gs_r.at[t], gr_r.at[d - 1], xpeer(d)))
    lhs = taps(uf, 8, 160)
    upd = []
    for d in (2, 1, 3, 0):
        t = (x + d) % XN
        gs_u[t] = dot(lhs, jnp.concatenate([w_upd[t], w_cx[t]], axis=1)).astype(BF)
        if d:
            upd.append(push(gs_u.at[t], gr_u.at[d - 1], xpeer(d)))
    sum_r = gs_r[x].astype(F32)
    landed(res)
    for d in range(3):
        sum_r = sum_r + gr_r[d].astype(F32)
    zs_r[...] = sum_r.astype(BF)
    zr = push(zs_r, zr_r, partner)
    sum_u = gs_u[x].astype(F32)
    landed(upd)
    for d in range(3):
        sum_u = sum_u + gr_u[d].astype(F32)
    zs_u[...] = sum_u.astype(BF)
    zu = push(zs_u, zr_u, partner)

    for e in range(3):
        ut[e * 128:e * 128 + 128, :] = uf[(e + 3) * 8:(e + 3) * 8 + 128, :].T.astype(BF)
    landed(pair)
    biases = bz_s[...] + bz_r[...]
    for lo, mine, theirs in (
        (0, halo_l[:, 128:], near_l[...]), (32, f_ref[:, 128:], far[...]), (160, halo_r[:, 128:], near_r[...])
    ):
        mine, theirs = mine.astype(F32), theirs.astype(F32)
        block_0 = jnp.where(first_z, mine, theirs)
        block_1 = jnp.where(first_z, theirs, mine)
        at = slot_a(mine.shape)
        hp[lo:lo + mine.shape[0], :] = jnp.where(at, swap(block_0), block_1)
        cp[lo:lo + mine.shape[0], :] = jnp.where(at, block_0, swap(block_1))
    pair_w.wait_recv()
    arrange(pair_hidden, w_ch)

    zr.wait_recv()
    r = jax.nn.sigmoid(sum_r + zr_r[...].astype(F32) + biases[1:2, :])
    gp = (r * hp[8:184, :]).astype(BF).astype(F32)
    gpf[...] = gp

    lhs = taps(gpf, 0, 160)
    cand = []
    for d in (2, 1, 3, 0):
        t = (x + d) % XN
        cs[t] = dot(lhs, w_ch[t]).astype(BF)
        if d:
            cand.append(push(cs.at[t], cr.at[d - 1], xpeer(d)))
    own_v = jnp.where(slot_a((176, 128)), uf[8:184, :], own_b(gp))
    for e in range(3):
        vt[e * 128:e * 128 + 128, :] = own_v[(e + 2) * 8:(e + 2) * 8 + 128].T.astype(BF)
    zu.wait_recv()
    sum_u = sum_u + zr_u[...].astype(F32)
    u = jax.nn.sigmoid(sum_u[:, :128] + biases[0:1, :])
    pre = sum_u[:, 128:] + biases[2:3, :] + cs[x].astype(F32)
    landed(cand)
    for d in range(3):
        pre = pre + cr[d].astype(F32)
    fresh = jnp.tanh(pre)
    h = hp[16:176, :]
    cot = cp[16:176, :]
    cg = (cot * u * (1.0 - fresh * fresh)).astype(BF)
    g1c[x] = cg
    got_c = [push(g1c.at[x], g1c.at[x], xpeer(d)) for d in (2, 1, 3)]
    ug = (cot * (fresh - h) * u * (1.0 - u)).astype(BF)
    g1u[x] = ug
    got_u = [push(g1u.at[x], g1u.at[x], xpeer(d)) for d in (2, 1, 3)]
    direct = (cot * (1.0 - u))[16:144]
    hn = ((1.0 - u) * h + u * fresh)[16:144]
    field_ref[:, :128] = own_a(hn).astype(BF)
    sum_c = jnp.sum(cg[16:144].astype(F32), axis=0, keepdims=True)
    sum_g = jnp.sum(ug[16:144].astype(F32), axis=0, keepdims=True)

    landed(got_c)
    grads = tiles(g1c)
    gg = shifted(dot_nt(grads, tiles(w_ch)), 0, 144)
    r_near = r[16:160]
    rt = (gg * hp[24:168, :] * r_near * (1.0 - r_near)).astype(BF).astype(F32)
    edge = jnp.zeros((8, 128), F32)
    g2[x] = jnp.concatenate([edge, rt, edge], axis=0).astype(BF)
    got_r = [push(g2.at[x], g2.at[x], xpeer(d)) for d in (2, 1, 3)]
    sum_q = jnp.sum(rt[8:136], axis=0, keepdims=True)
    bs[...] = jnp.where(row == 0, sum_g, jnp.where(row == 1, sum_q, jnp.where(row == 2, sum_c, 0.0)))
    bias1 = [push(bs, br.at[d - 1], mpeer(d)) for d in range(1, 8)]

    low = lax.broadcasted_iota(jnp.int32, (64, 128), 1) < 64

    def weight_grad(left_ref, grad_ref, out_ref, start):
        left_rows = left_ref[...]
        for q in range(2):
            rhs = jnp.concatenate([grad_ref[2 * q, 16:144, :], grad_ref[2 * q + 1, 16:144, :]], axis=1)
            product = dot(left_rows, rhs)
            for e in range(3):
                t0 = product[e * 128:e * 128 + 128, :128]
                t1 = product[e * 128:e * 128 + 128, 128:]
                slabs = (
                    jnp.where(low, t0[64:], t0[:64]),
                    jnp.where(low, t1[64:], t1[:64]),
                    jnp.where(low, t0[:64] + roll(t0[64:], 64), t1[64:] + roll(t1[:64], 64)),
                )
                for k, slab in enumerate(slabs):
                    n = (start + e * 6 + q * 3 + k) * 64
                    out_ref[n:n + 64, :] = slab.astype(BF)

    def chunk(t, rows):
        return pl.ds(pl.multiple_of(t * rows, 16), rows)

    weight_grad(vt, g1c, blob_a, 0)
    landed(got_u)
    weight_grad(ut, g1u, blob_a, 18)
    half = [push(blob_a.at[chunk(t * CN + 1 - core, 288), :], core_a.at[t], other_core) for t in range(4)]
    total = shifted(dot_nt(grads, tiles(w_cx)), 8, 128) + shifted(dot_nt(tiles(g1u), tiles(w_upd)), 8, 128)
    landed(half)
    for t in range(4):
        mid_a[t] = (blob_a[chunk(t * CN + core, 288), :].astype(F32) + core_a[t].astype(F32)).astype(BF)
    over_y = [push(mid_a.at[(yy + d) % YN], y_a.at[d - 1], ypeer(d)) for d in (2, 1, 3)]

    landed(got_r)
    weight_grad(ut, g2, blob_r, 0)
    over_m = [push(blob_r.at[chunk((m + d) % 8, 144), :], m_r.at[d - 1], mpeer(d)) for d in range(1, 8)]
    total = total + shifted(dot_nt(tiles(g2), tiles(w_res)), 8, 128)
    hidden = own_b(direct + gg[8:136] * r[24:152])
    field_ref[:, 128:] = jnp.where(slot_a((128, 128)), total, hidden + total).astype(BF)

    acc = mid_a[yy].astype(F32)
    landed(over_y)
    for d in range(3):
        acc = acc + y_a[d].astype(F32)
    for p in range(6):
        zs_a[p] = acc[p * 48:p * 48 + 48].astype(BF)
    for p in (6, 7):
        zs_a[p] = jnp.zeros((48, 128), BF)
    over_za = [push(zs_a.at[(zl + d) % ZL], zq_a.at[d - 1], lpeer(d)) for d in range(1, 8)]
    b1 = bs[...]
    landed(bias1)
    for d in range(7):
        b1 = b1 + br[d]
    bs2[...] = b1
    bias2 = [push(bs2, br2.at[d - 1], lpeer(d)) for d in range(1, 8)]
    acc = blob_r[chunk(m, 144), :].astype(F32)
    landed(over_m)
    for d in range(7):
        acc = acc + m_r[d].astype(F32)
    for p in range(4):
        zs_b[p] = acc[p * 32:p * 32 + 32].astype(BF)
    zs_b[4] = jnp.concatenate([acc[128:144], jnp.zeros((16, 128), F32)], axis=0).astype(BF)
    for p in (5, 6, 7):
        zs_b[p] = jnp.zeros((32, 128), BF)
    over_zb = [push(zs_b.at[(zl + d) % ZL], zq_b.at[d - 1], lpeer(d)) for d in range(1, 8)]

    def own_sum(mine, came, copies, out):
        value = mine[zl].astype(F32)
        landed(copies)
        for d in range(7):
            value = value + came[d].astype(F32)
        out[zl] = value.astype(BF)
        return [push(out.at[zl], out.at[zl], lpeer(d)) for d in range(1, 8)]

    back_a = own_sum(zs_a, zq_a, over_za, zf_a)
    back_b = own_sum(zs_b, zq_b, over_zb, zf_b)

    def spread(fin):
        to_y = [push(fin.at[m], fin.at[m], ypeer(d)) for d in (2, 1, 3)]
        return to_y, [push(fin.at[m], fin.at[m], other_core)]

    def forward(fin, to_y, rest):
        for copy, d in zip(to_y, (2, 1, 3)):
            copy.wait_recv()
            at = ((yy + YN - d) % YN) * CN + core
            rest.append(push(fin.at[at], fin.at[at], other_core))

    landed(back_a)
    for p in range(6):
        fin_a[m, p * 48:p * 48 + 48, :] = zf_a[p]
    to_ya, rest_a = spread(fin_a)
    landed(back_b)
    for p in range(4):
        fin_r[m, p * 32:p * 32 + 32, :] = zf_b[p]
    fin_r[m, 128:144, :] = zf_b[4, 0:16, :]
    to_yr, rest_r = spread(fin_r)
    b2 = bs2[...]
    landed(bias2)
    for d in range(7):
        b2 = b2 + br2[d]
    bias_ref[...] = own_a(b2)
    forward(fin_a, to_ya, rest_a)
    forward(fin_r, to_yr, rest_r)
    landed(rest_a)
    landed(rest_r)
    for copy in sends:
        copy.wait_send()


def finish(
    reset_ref, field_ref, fin_a, fin_r, bias_ref, q5_ref, pm_ref,
    hn_ref, gx_ref, gh_ref, wgg_ref, gb_ref, wgc_ref, cb_ref,
):
    rows = dot(pm_ref[...], field_ref[...])
    for i in range(2):
        hn_ref[:, i] = rows[:, i * 64:i * 64 + 32].reshape(8, 16, 32).astype(BF)
        gx_ref[:, i] = rows[:, 128 + i * 64:160 + i * 64].reshape(8, 16, 32).astype(BF)
        value = rows[:, 160 + i * 64:192 + i * 64].reshape(8, 16, 32)
        for b in range(8):
            gh_ref[b, i] = (value[b] * (1 - reset_ref[b]).astype(F32)).astype(BF)
    sums = bias_ref[...]
    sums = sums + roll(sums, 64)
    gb_ref[...] = sums[0:2, 0:32]
    cb_ref[...] = sums[2:3, 0:32]

    def slab(fin, size, step, n):
        pieces = [fin[r // size, r % size:r % size + step, :] for r in range(n * 64, n * 64 + 64, step)]
        return jnp.concatenate(pieces, axis=0)

    def put(gate, a, e, value):
        for s in range(2):
            part = value[s * 32:s * 32 + 32]
            if gate is None:
                wgc_ref[s, a, e] = part
            else:
                wgg_ref[s, a, e, :, gate, :] = part

    q5 = q5_ref[...]
    for gate, fin, size, step, start in (
        (None, fin_a, 288, 32, 0), (0, fin_a, 288, 32, 18), (1, fin_r, 144, 16, 0)
    ):
        def get(e, q, k):
            return slab(fin, size, step, start + e * 6 + q * 3 + k)

        outer = jnp.concatenate(
            [
                jnp.concatenate([get(e, q, k) for q in range(2) for k in range(2)], axis=1)
                for e in range(3)
            ],
            axis=0,
        )
        outer = dot(outer, q5)
        for e in range(3):
            at = slice(e * 64, e * 64 + 64)
            put(gate, 2, e, outer[at, :256])
            put(gate, 0, e, outer[at, 256:])
            inner = jnp.concatenate([get(e, q, 2) for q in range(2)], axis=1)
            put(gate, 1, e, inner.astype(F32))


def per_device(x_in, h_prev, reset, w_gate, gate_bias, w_cand, cand_bias, cotangent):
    def bf(*shape):
        return pltpu.VMEM(shape, BF)

    def f32(*shape):
        return pltpu.VMEM(shape, F32)

    scratch = [
        bf(128, 256), bf(32, 256), bf(32, 256), f32(192, 128), bf(32, 128), bf(32, 128), bf(128, 128),
        f32(192, 128), f32(192, 128), bf(2, 288, 256),
        bf(4, 384, 128), bf(4, 384, 128), bf(4, 384, 128), bf(4, 384, 128),
        f32(8, 128), f32(8, 128), bf(4, 176, 128), bf(3, 176, 128), bf(4, 160, 256), bf(3, 160, 256),
        bf(176, 128), bf(176, 128), bf(160, 256), bf(160, 256), f32(176, 128), bf(4, 160, 128), bf(3, 160, 128),
        bf(4, 160, 128), bf(4, 160, 128), bf(4, 160, 128), bf(384, 128), bf(384, 128),
        bf(2304, 128), bf(1152, 128), bf(4, 288, 128), bf(4, 288, 128), bf(3, 288, 128), bf(7, 144, 128),
        bf(8, 48, 128), bf(7, 48, 128), bf(8, 48, 128), bf(8, 32, 128), bf(7, 32, 128), bf(8, 32, 128),
        f32(8, 128), f32(7, 8, 128), f32(8, 128), f32(7, 8, 128),
        pltpu.SemaphoreType.DMA((COPIES,)), pltpu.SemaphoreType.DMA((COPIES,)),
    ]
    q5 = jnp.asarray(block_transpose(4, 2, 64), BF)
    rows_in = jnp.asarray(row_order(), BF)
    rows_out = jnp.asarray(row_order().T, BF)
    near = lambda v: v.transpose(1, 2, 3, 0)
    smem = pl.BlockSpec(memory_space=pltpu.SMEM)
    whole = pl.BlockSpec(memory_space=pltpu.VMEM)
    field, fin_a, fin_r, bias = pl.pallas_call(
        kernel,
        out_shape=(
            jax.ShapeDtypeStruct((128, 256), BF),
            jax.ShapeDtypeStruct((8, 288, 128), BF),
            jax.ShapeDtypeStruct((8, 144, 128), BF),
            jax.ShapeDtypeStruct((8, 128), F32),
        ),
        in_specs=[smem] + [whole] * 9,
        out_specs=[whole] * 4,
        scratch_shapes=scratch,
        compiler_params=pltpu.CompilerParams(
            collective_id=0, has_side_effects=True, vmem_limit_bytes=48 * 1024 * 1024
        ),
        cost_estimate=pl.CostEstimate(flops=1_000_000_000, bytes_accessed=8_000_000, transcendentals=100_000),
    )(
        reset, near(x_in), near(h_prev), near(cotangent), w_gate.reshape(576, 512), w_cand.reshape(576, 256),
        gate_bias, cand_bias.reshape(1, 32), q5, rows_in,
    )
    shape = jax.ShapeDtypeStruct((8, 2, 16, 32), BF)
    h_new, grad_x, grad_h, wgg, gb, wgc, cb = pl.pallas_call(
        finish,
        out_shape=(
            shape, shape, shape,
            jax.ShapeDtypeStruct(w_gate.shape, F32), jax.ShapeDtypeStruct((2, 32), F32),
            jax.ShapeDtypeStruct(w_cand.shape, F32), jax.ShapeDtypeStruct((1, 32), F32),
        ),
        in_specs=[smem] + [whole] * 6,
        out_specs=[whole] * 7,
        compiler_params=pltpu.CompilerParams(vmem_limit_bytes=32 * 1024 * 1024),
    )(reset, field, fin_a, fin_r, bias, q5, rows_out)
    back = lambda v: v.transpose(3, 0, 1, 2)
    return back(h_new), back(grad_x), back(grad_h), wgg, gb, wgc, cb.reshape(32)


def solution(mesh):
    field = P("filt", None, None, "wedge")
    in_specs = (
        field, field, P(), P(None, None, None, "filt", None, None), P(None, "filt"),
        P(None, None, None, "filt", None), P("filt"), field,
    )
    out_specs = (
        field, field, field, P(None, None, None, "filt", None, None), P(None, "filt"),
        P(None, None, None, "filt", None), P("filt"),
    )
    return jax.shard_map(per_device, mesh=mesh, in_specs=in_specs, out_specs=out_specs, check_vma=False)
```

```python
import numpy as np
import jax
import jax.numpy as jnp
from jax import lax
from jax.experimental import pallas as pl
from jax.experimental.pallas import tpu as pltpu
from jax.sharding import PartitionSpec as P

XN, ZH, YN, ZL, CN = 4, 2, 4, 8, 2
WEDGES = YN * ZL * CN
COPIES = 128
MESH = pl.DeviceIdType.MESH
BF = jnp.bfloat16
F32 = jnp.float32
NT = (((1,), (1,)), ((), ()))


def block_transpose(first, second, third):
    size = first * second * third
    order = np.arange(size).reshape(first, second, third).transpose(1, 0, 2).reshape(-1)
    matrix = np.zeros((size, size), np.float32)
    matrix[order, np.arange(size)] = 1.0
    return matrix


def row_order():
    order = np.arange(128).reshape(8, 16).T.reshape(-1)
    matrix = np.zeros((128, 128), np.float32)
    matrix[np.arange(128), order] = 1.0
    return matrix


def roll(v, shift):
    return pltpu.roll(v, shift, 1)


def slot_a(shape):
    return lax.broadcasted_iota(jnp.int32, shape, 1) % 64 < 32


def swap(v):
    return jnp.where(slot_a(v.shape), roll(v, 96), roll(v, 32))


def dot(a, b):
    return jnp.dot(a, b, preferred_element_type=F32)


def dot_nt(a, b):
    return lax.dot_general(a, b, NT, preferred_element_type=F32)


def tiles(ref):
    return jnp.concatenate([ref[t] for t in range(4)], axis=1)


def taps(ref, start, rows):
    return jnp.concatenate([ref[start + e * 8:start + e * 8 + rows, :].astype(BF) for e in range(3)], axis=1)


def shifted(v, start, rows):
    out = None
    for e in range(3):
        part = v[start + (2 - e) * 8:start + (2 - e) * 8 + rows, e * 128:e * 128 + 128]
        out = part if out is None else out + part
    return out


def kernel(
    reset_ref, x_ref, h_ref, ct_ref, wg_ref, wc_ref, gb_ref, cb_ref, q5_ref, pm_ref,
    field_ref, fin_a, fin_r, bias_ref,
    f_ref, halo_l, halo_r, uf, near_l, near_r, far, hp, cp, wq, wch, w_upd, w_res, w_cx, w_ch,
    bz_s, bz_r, gs_ri, gr_ri, gs_ui, gr_ui, gs_re, gr_re, gs_ue, gr_ue,
    zs_ri, zr_ri, zs_ui, zr_ui, zs_re, zr_re, zs_ue, zr_ue, gpf, cs, cr,
    g1c, g1u, g2, ut, vt, blob_a, blob_r, core_a, mid_a, y_a, m_r,
    zs_a, zq_a, zf_a, zs_b, zq_b, zf_b, bs, br, bs2, br2,
    send_sems, recv_sems, up_s, up_r, down_s, down_r,
):
    w = lax.axis_index("wedge")
    f = lax.axis_index("filt")
    x, zh = f // ZH, f % ZH
    core, zl, yy = w % CN, (w // CN) % ZL, w // (CN * ZL)
    m = yy * CN + core
    first_z = zh == 0
    fp = x * ZH + (1 - zh)
    after, before = (w + 1) % WEDGES, (w + WEDGES - 1) % WEDGES

    def xpeer(d):
        return (w, ((x + d) % XN) * ZH + zh)

    def at_y(t, c):
        return (t * ZL + zl) * CN + c, f

    def mpeer(d):
        t = (m + d) % 8
        return at_y(t // CN, t % CN)

    def ypeer(d):
        return at_y((yy + d) % YN, core)

    def lpeer(d):
        return (yy * ZL + (zl + d + ZL) % ZL) * CN + core, f

    partner = (w, fp)
    other_core = at_y(yy, 1 - core)
    peers = [(after, f), (before, f), (after, fp), (before, fp), partner] + [xpeer(d) for d in (1, 2, 3)]
    peers += [mpeer(d) for d in range(1, 8)] + [lpeer(d) for d in range(1, 8)]
    barrier = pltpu.get_barrier_semaphore()
    for peer in peers:
        pl.semaphore_signal(barrier, inc=1, device_id=peer, device_id_type=MESH)

    def own_a(v):
        return jnp.where(first_z, v, swap(v))

    def own_b(v):
        return jnp.where(first_z, swap(v), v)

    order = pm_ref[...]
    kept = jnp.concatenate(
        [h_ref[b:b + 1].astype(F32) * (1 - reset_ref[b]).astype(F32) for b in range(8)], axis=0
    )
    near, wide = [], []
    for i in range(2):
        hidden = kept[:, i].reshape(128, 32)
        near += [x_ref[:, i].reshape(128, 32).astype(F32), hidden]
        wide += [ct_ref[:, i].reshape(128, 32).astype(F32), hidden]
    own_u = dot(order, jnp.concatenate(near, axis=1).astype(BF))
    own_c = dot(order, jnp.concatenate(wide, axis=1).astype(BF))
    f_ref[:, :128] = own_u.astype(BF)
    f_ref[:, 128:] = own_c.astype(BF)
    uf[32:160, :] = own_u
    row = lax.broadcasted_iota(jnp.int32, (8, 128), 0)
    bias_rows = [jnp.concatenate([v] * 4, axis=1) for v in (gb_ref[0:1, :], gb_ref[1:2, :], cb_ref[...])]
    bias_rows = jnp.where(row == 0, bias_rows[0], jnp.where(row == 1, bias_rows[1], bias_rows[2]))
    bz_s[...] = jnp.where(slot_a((8, 128)) == first_z, bias_rows, 0.0)
    q5 = q5_ref[...]

    def arrange(nat, out_ref):
        lhs = jnp.concatenate(
            [
                jnp.concatenate([nat(a, e) for a in (ip + 1, ip)], axis=1)
                for e in range(3)
                for ip in range(2)
            ],
            axis=0,
        )
        out = dot_nt(lhs, q5).astype(BF)
        for t in range(4):
            out_ref[t] = out[:, t * 128:t * 128 + 128]

    def both(gate):
        def nat(a, e):
            return jnp.concatenate([wg_ref[((s * 3 + a) * 3 + e) * 32:((s * 3 + a) * 3 + e) * 32 + 32, gate * 256:gate * 256 + 256] for s in range(2)], axis=0)

        return nat

    def input_only(a, e):
        at = (a * 3 + e) * 32
        return jnp.concatenate([wc_ref[at:at + 32, :], jnp.zeros((32, 256), BF)], axis=0)

    def pair_hidden(a, e):
        at = (a * 3 + e) * 32
        return jnp.concatenate([wch[0, at:at + 32, :], wch[1, at:at + 32, :]], axis=0)

    arrange(both(1), w_res)
    arrange(both(0), w_upd)
    arrange(input_only, w_cx)
    pl.semaphore_wait(barrier, len(peers))

    sends = []

    def push(src, dst, peer):
        at = len(sends)
        copy = pltpu.make_async_remote_copy(
            src_ref=src, dst_ref=dst, send_sem=send_sems.at[at], recv_sem=recv_sems.at[at],
            device_id=peer, device_id_type=MESH,
        )
        copy.start()
        sends.append(copy)
        return copy

    def landed(copies):
        for copy in copies:
            copy.wait_recv()

    right, left = pl.ds(96, 32), pl.ds(0, 32)
    second = pl.ds(128, 128)
    halo = [
        push(f_ref.at[right, :], halo_l, (after, f)),
        push(f_ref.at[left, :], halo_r, (before, f)),
    ]
    pair = [
        push(f_ref.at[right, second], near_l, (after, fp)),
        push(f_ref.at[left, second], near_r, (before, fp)),
        push(f_ref.at[:, second], far, partner),
        push(bz_s, bz_r, partner),
    ]
    part = pl.multiple_of(288 + (m % 6) * 48, 16)
    pair_w = push(wc_ref.at[pl.ds(part, 48), :], wq.at[m], partner)
    def partial(lhs, gs_r, gr_r, gs_u, gr_u):
        res, upd = [], []
        for d in (2, 1, 3, 0):
            t = (x + d) % XN
            gs_r[t] = dot(lhs, w_res[t]).astype(BF)
            if d:
                res.append(push(gs_r.at[t], gr_r.at[d - 1], xpeer(d)))
        for d in (2, 1, 3, 0):
            t = (x + d) % XN
            gs_u[t] = dot(lhs, jnp.concatenate([w_upd[t], w_cx[t]], axis=1)).astype(BF)
            if d:
                upd.append(push(gs_u.at[t], gr_u.at[d - 1], xpeer(d)))
        return res, upd

    def summed(gs, gr, copies, zs, zr):
        value = gs[x].astype(F32)
        landed(copies)
        for d in range(3):
            value = value + gr[d].astype(F32)
        zs[...] = value.astype(BF)
        return value, push(zs, zr, partner)

    res_i, upd_i = partial(taps(uf, 32, 112), gs_ri, gr_ri, gs_ui, gr_ui)
    sum_ri, zri = summed(gs_ri, gr_ri, res_i, zs_ri, zr_ri)
    landed(halo)
    uf[0:32, :] = halo_l[:, :128].astype(F32)
    uf[160:192, :] = halo_r[:, :128].astype(F32)
    lhs = jnp.concatenate([taps(uf, 0, 32), taps(uf, 144, 32)], axis=0)
    res_e, upd_e = partial(lhs, gs_re, gr_re, gs_ue, gr_ue)
    sum_re, zre = summed(gs_re, gr_re, res_e, zs_re, zr_re)
    sum_ui, zui = summed(gs_ui, gr_ui, upd_i, zs_ui, zr_ui)
    sum_ue, zue = summed(gs_ue, gr_ue, upd_e, zs_ue, zr_ue)
    pair_w.wait_recv()
    shares = [push(wq.at[m], wq.at[m], mpeer(d)) for d in range(1, 8)]

    for e in range(3):
        ut[e * 128:e * 128 + 128, :] = uf[(e + 3) * 8:(e + 3) * 8 + 128, :].T.astype(BF)
    landed(pair)
    biases = bz_s[...] + bz_r[...]
    for lo, mine, theirs in (
        (0, halo_l[:, 128:], near_l[...]), (32, f_ref[:, 128:], far[...]), (160, halo_r[:, 128:], near_r[...])
    ):
        mine, theirs = mine.astype(F32), theirs.astype(F32)
        block_0 = jnp.where(first_z, mine, theirs)
        block_1 = jnp.where(first_z, theirs, mine)
        at = slot_a(mine.shape)
        hp[lo:lo + mine.shape[0], :] = jnp.where(at, swap(block_0), block_1)
        cp[lo:lo + mine.shape[0], :] = jnp.where(at, block_0, swap(block_1))
    landed(shares)
    wch[zh] = wc_ref[288:576, :]
    for k in range(6):
        wch[1 - zh, k * 48:k * 48 + 48, :] = wq[k]
    arrange(pair_hidden, w_ch)

    def joined(edge, inner):
        return jnp.concatenate([edge[:32], inner, edge[32:]], axis=0)

    landed([zri, zre])
    sum_r = joined(sum_re + zr_re[...].astype(F32), sum_ri + zr_ri[...].astype(F32))
    r = jax.nn.sigmoid(sum_r + biases[1:2, :])
    gp = (r * hp[8:184, :]).astype(BF).astype(F32)
    gpf[...] = gp

    lhs = taps(gpf, 0, 160)
    cand = []
    for d in (2, 1, 3, 0):
        t = (x + d) % XN
        cs[t] = dot(lhs, w_ch[t]).astype(BF)
        if d:
            cand.append(push(cs.at[t], cr.at[d - 1], xpeer(d)))
    own_v = jnp.where(slot_a((176, 128)), uf[8:184, :], own_b(gp))
    for e in range(3):
        vt[e * 128:e * 128 + 128, :] = own_v[(e + 2) * 8:(e + 2) * 8 + 128].T.astype(BF)
    landed([zui, zue])
    sum_u = joined(sum_ue + zr_ue[...].astype(F32), sum_ui + zr_ui[...].astype(F32))[8:168]
    u = jax.nn.sigmoid(sum_u[:, :128] + biases[0:1, :])
    pre = sum_u[:, 128:] + biases[2:3, :] + cs[x].astype(F32)
    landed(cand)
    for d in range(3):
        pre = pre + cr[d].astype(F32)
    fresh = jnp.tanh(pre)
    h = hp[16:176, :]
    cot = cp[16:176, :]
    cg = (cot * u * (1.0 - fresh * fresh)).astype(BF)
    g1c[x] = cg
    got_c = [push(g1c.at[x], g1c.at[x], xpeer(d)) for d in (2, 1, 3)]
    ug = (cot * (fresh - h) * u * (1.0 - u)).astype(BF)
    g1u[x] = ug
    got_u = [push(g1u.at[x], g1u.at[x], xpeer(d)) for d in (2, 1, 3)]
    direct = (cot * (1.0 - u))[16:144]
    hn = ((1.0 - u) * h + u * fresh)[16:144]
    field_ref[:, :128] = own_a(hn).astype(BF)
    sum_c = jnp.sum(cg[16:144].astype(F32), axis=0, keepdims=True)
    sum_g = jnp.sum(ug[16:144].astype(F32), axis=0, keepdims=True)

    landed(got_c)
    grads = tiles(g1c)
    gg = shifted(dot_nt(grads, tiles(w_ch)), 0, 144)
    r_near = r[16:160]
    rt = (gg * hp[24:168, :] * r_near * (1.0 - r_near)).astype(BF).astype(F32)
    edge = jnp.zeros((8, 128), F32)
    g2[x] = jnp.concatenate([edge, rt, edge], axis=0).astype(BF)
    got_r = [push(g2.at[x], g2.at[x], xpeer(d)) for d in (2, 1, 3)]
    sum_q = jnp.sum(rt[8:136], axis=0, keepdims=True)
    bs[...] = jnp.where(row == 0, sum_g, jnp.where(row == 1, sum_q, jnp.where(row == 2, sum_c, 0.0)))
    bias1 = [push(bs, br.at[d - 1], mpeer(d)) for d in range(1, 8)]

    low = lax.broadcasted_iota(jnp.int32, (64, 128), 1) < 64

    def weight_grad(left_ref, grad_ref, out_ref, start):
        left_rows = left_ref[...]
        for q in range(2):
            rhs = jnp.concatenate([grad_ref[2 * q, 16:144, :], grad_ref[2 * q + 1, 16:144, :]], axis=1)
            product = dot(left_rows, rhs)
            for e in range(3):
                t0 = product[e * 128:e * 128 + 128, :128]
                t1 = product[e * 128:e * 128 + 128, 128:]
                slabs = (
                    jnp.where(low, t0[64:], t0[:64]),
                    jnp.where(low, t1[64:], t1[:64]),
                    jnp.where(low, t0[:64] + roll(t0[64:], 64), t1[64:] + roll(t1[:64], 64)),
                )
                for k, slab in enumerate(slabs):
                    n = (start + e * 6 + q * 3 + k) * 64
                    out_ref[n:n + 64, :] = slab.astype(BF)

    def chunk(t, rows):
        return pl.ds(pl.multiple_of(t * rows, 16), rows)

    weight_grad(vt, g1c, blob_a, 0)
    landed(got_u)
    weight_grad(ut, g1u, blob_a, 18)
    half = [push(blob_a.at[chunk(t * CN + 1 - core, 288), :], core_a.at[t], other_core) for t in range(4)]
    total = shifted(dot_nt(grads, tiles(w_cx)), 8, 128) + shifted(dot_nt(tiles(g1u), tiles(w_upd)), 8, 128)
    landed(half)
    for t in range(4):
        mid_a[t] = (blob_a[chunk(t * CN + core, 288), :].astype(F32) + core_a[t].astype(F32)).astype(BF)
    over_y = [push(mid_a.at[(yy + d) % YN], y_a.at[d - 1], ypeer(d)) for d in (2, 1, 3)]

    landed(got_r)
    weight_grad(ut, g2, blob_r, 0)
    over_m = [push(blob_r.at[chunk((m + d) % 8, 144), :], m_r.at[d - 1], mpeer(d)) for d in range(1, 8)]
    total = total + shifted(dot_nt(tiles(g2), tiles(w_res)), 8, 128)
    hidden = own_b(direct + gg[8:136] * r[24:152])
    field_ref[:, 128:] = jnp.where(slot_a((128, 128)), total, hidden + total).astype(BF)

    def reduce_z(owners, mine, came, out, which):
        def copy(src, dst, send, recv, z):
            return pltpu.make_async_remote_copy(
                src_ref=src, dst_ref=dst, send_sem=send, recv_sem=recv, device_id=lpeer(z - zl), device_id_type=MESH
            )

        def up(i, s, p):
            return copy(mine.at[i], came.at[s], up_s.at[which, i], up_r.at[which, s], p)

        def down(i, d, z):
            return copy(out.at[i], out.at[i], down_s.at[which, d - 1], down_r.at[which, i], z)

        for i, p in enumerate(owners):
            pl.when(zl != p)(up(i, zl, p).start)

        def own():
            for i, p in enumerate(owners):
                @pl.when(zl == p)
                def _():
                    value = mine[i].astype(F32)
                    for s in range(8):
                        if s != p:
                            up(i, s, p).wait_recv()
                            value = value + came[s].astype(F32)
                    out[i] = value.astype(BF)
                    for d in range(1, 8):
                        down(i, d, (p + d) % 8).start()

        def back():
            for i, p in enumerate(owners):
                pl.when(zl != p)(down(i, 1, p).wait_recv)

        def close():
            for i, p in enumerate(owners):
                @pl.when(zl != p)
                def _():
                    up(i, zl, p).wait_send()

                @pl.when(zl == p)
                def _():
                    for d in range(1, 8):
                        down(i, d, (p + d) % 8).wait_send()

        return own, back, close

    acc = mid_a[yy].astype(F32)
    landed(over_y)
    for d in range(3):
        acc = acc + y_a[d].astype(F32)
    for p in range(3):
        zs_a[p] = acc[p * 80:p * 80 + 80].astype(BF)
    zs_a[3] = jnp.concatenate([acc[240:288], jnp.zeros((32, 128), F32)], axis=0).astype(BF)
    own_za, back_za, close_za = reduce_z((2, 3, 4, 5), zs_a, zq_a, zf_a, 0)
    b1 = bs[...]
    landed(bias1)
    for d in range(7):
        b1 = b1 + br[d]
    bs2[...] = b1
    bias2 = [push(bs2, br2.at[d - 1], lpeer(d)) for d in range(1, 8)]
    acc = blob_r[chunk(m, 144), :].astype(F32)
    landed(over_m)
    for d in range(7):
        acc = acc + m_r[d].astype(F32)
    zs_b[0] = acc[0:80].astype(BF)
    zs_b[1] = jnp.concatenate([acc[80:144], jnp.zeros((16, 128), F32)], axis=0).astype(BF)
    own_zb, back_zb, close_zb = reduce_z((3, 4), zs_b, zq_b, zf_b, 1)
    own_za()
    own_zb()

    def spread(fin):
        to_y = [push(fin.at[m], fin.at[m], ypeer(d)) for d in (2, 1, 3)]
        return to_y, [push(fin.at[m], fin.at[m], other_core)]

    def forward(fin, to_y, rest):
        for copy, d in zip(to_y, (2, 1, 3)):
            copy.wait_recv()
            at = ((yy + YN - d) % YN) * CN + core
            rest.append(push(fin.at[at], fin.at[at], other_core))

    back_za()
    for p in range(3):
        fin_a[m, p * 80:p * 80 + 80, :] = zf_a[p]
    fin_a[m, 240:288, :] = zf_a[3, 0:48, :]
    to_ya, rest_a = spread(fin_a)
    back_zb()
    fin_r[m, 0:80, :] = zf_b[0]
    fin_r[m, 80:144, :] = zf_b[1, 0:64, :]
    to_yr, rest_r = spread(fin_r)
    b2 = bs2[...]
    landed(bias2)
    for d in range(7):
        b2 = b2 + br2[d]
    bias_ref[...] = own_a(b2)
    forward(fin_a, to_ya, rest_a)
    forward(fin_r, to_yr, rest_r)
    landed(rest_a)
    landed(rest_r)
    close_za()
    close_zb()
    for copy in sends:
        copy.wait_send()


def finish(
    reset_ref, field_ref, fin_a, fin_r, bias_ref, q5_ref, pm_ref,
    hn_ref, gx_ref, gh_ref, wgg_ref, gb_ref, wgc_ref, cb_ref,
):
    rows = dot(pm_ref[...], field_ref[...])
    for i in range(2):
        hn_ref[:, i] = rows[:, i * 64:i * 64 + 32].reshape(8, 16, 32).astype(BF)
        gx_ref[:, i] = rows[:, 128 + i * 64:160 + i * 64].reshape(8, 16, 32).astype(BF)
        value = rows[:, 160 + i * 64:192 + i * 64].reshape(8, 16, 32)
        for b in range(8):
            gh_ref[b, i] = (value[b] * (1 - reset_ref[b]).astype(F32)).astype(BF)
    sums = bias_ref[...]
    sums = sums + roll(sums, 64)
    gb_ref[...] = sums[0:2, 0:32]
    cb_ref[...] = sums[2:3, 0:32]

    def slab(fin, size, step, n):
        pieces = [fin[r // size, r % size:r % size + step, :] for r in range(n * 64, n * 64 + 64, step)]
        return jnp.concatenate(pieces, axis=0)

    def put(gate, a, e, value):
        for s in range(2):
            part = value[s * 32:s * 32 + 32]
            if gate is None:
                wgc_ref[s, a, e] = part
            else:
                wgg_ref[s, a, e, :, gate, :] = part

    q5 = q5_ref[...]
    for gate, fin, size, step, start in (
        (None, fin_a, 288, 32, 0), (0, fin_a, 288, 32, 18), (1, fin_r, 144, 16, 0)
    ):
        def get(e, q, k):
            return slab(fin, size, step, start + e * 6 + q * 3 + k)

        outer = jnp.concatenate(
            [
                jnp.concatenate([get(e, q, k) for q in range(2) for k in range(2)], axis=1)
                for e in range(3)
            ],
            axis=0,
        )
        outer = dot(outer, q5)
        for e in range(3):
            at = slice(e * 64, e * 64 + 64)
            put(gate, 2, e, outer[at, :256])
            put(gate, 0, e, outer[at, 256:])
            inner = jnp.concatenate([get(e, q, 2) for q in range(2)], axis=1)
            put(gate, 1, e, inner.astype(F32))


def per_device(x_in, h_prev, reset, w_gate, gate_bias, w_cand, cand_bias, cotangent):
    def bf(*shape):
        return pltpu.VMEM(shape, BF)

    def f32(*shape):
        return pltpu.VMEM(shape, F32)

    scratch = [
        bf(128, 256), bf(32, 256), bf(32, 256), f32(192, 128), bf(32, 128), bf(32, 128), bf(128, 128),
        f32(192, 128), f32(192, 128), bf(8, 48, 256), bf(2, 288, 256),
        bf(4, 384, 128), bf(4, 384, 128), bf(4, 384, 128), bf(4, 384, 128),
        f32(8, 128), f32(8, 128), bf(4, 112, 128), bf(3, 112, 128), bf(4, 112, 256), bf(3, 112, 256),
        bf(4, 64, 128), bf(3, 64, 128), bf(4, 64, 256), bf(3, 64, 256),
        bf(112, 128), bf(112, 128), bf(112, 256), bf(112, 256), bf(64, 128), bf(64, 128), bf(64, 256), bf(64, 256),
        f32(176, 128), bf(4, 160, 128), bf(3, 160, 128),
        bf(4, 160, 128), bf(4, 160, 128), bf(4, 160, 128), bf(384, 128), bf(384, 128),
        bf(2304, 128), bf(1152, 128), bf(4, 288, 128), bf(4, 288, 128), bf(3, 288, 128), bf(7, 144, 128),
        bf(4, 80, 128), bf(8, 80, 128), bf(4, 80, 128), bf(2, 80, 128), bf(8, 80, 128), bf(2, 80, 128),
        f32(8, 128), f32(7, 8, 128), f32(8, 128), f32(7, 8, 128),
        pltpu.SemaphoreType.DMA((COPIES,)), pltpu.SemaphoreType.DMA((COPIES,)),
        pltpu.SemaphoreType.DMA((2, 4)), pltpu.SemaphoreType.DMA((2, 8)),
        pltpu.SemaphoreType.DMA((2, 7)), pltpu.SemaphoreType.DMA((2, 4)),
    ]
    q5 = jnp.asarray(block_transpose(4, 2, 64), BF)
    rows_in = jnp.asarray(row_order(), BF)
    rows_out = jnp.asarray(row_order().T, BF)
    near = lambda v: v.transpose(1, 2, 3, 0)
    smem = pl.BlockSpec(memory_space=pltpu.SMEM)
    whole = pl.BlockSpec(memory_space=pltpu.VMEM)
    field, fin_a, fin_r, bias = pl.pallas_call(
        kernel,
        out_shape=(
            jax.ShapeDtypeStruct((128, 256), BF),
            jax.ShapeDtypeStruct((8, 288, 128), BF),
            jax.ShapeDtypeStruct((8, 144, 128), BF),
            jax.ShapeDtypeStruct((8, 128), F32),
        ),
        in_specs=[smem] + [whole] * 9,
        out_specs=[whole] * 4,
        scratch_shapes=scratch,
        compiler_params=pltpu.CompilerParams(
            collective_id=0, has_side_effects=True, vmem_limit_bytes=48 * 1024 * 1024
        ),
        cost_estimate=pl.CostEstimate(flops=1_000_000_000, bytes_accessed=8_000_000, transcendentals=100_000),
    )(
        reset, near(x_in), near(h_prev), near(cotangent), w_gate.reshape(576, 512), w_cand.reshape(576, 256),
        gate_bias, cand_bias.reshape(1, 32), q5, rows_in,
    )
    shape = jax.ShapeDtypeStruct((8, 2, 16, 32), BF)
    h_new, grad_x, grad_h, wgg, gb, wgc, cb = pl.pallas_call(
        finish,
        out_shape=(
            shape, shape, shape,
            jax.ShapeDtypeStruct(w_gate.shape, F32), jax.ShapeDtypeStruct((2, 32), F32),
            jax.ShapeDtypeStruct(w_cand.shape, F32), jax.ShapeDtypeStruct((1, 32), F32),
        ),
        in_specs=[smem] + [whole] * 6,
        out_specs=[whole] * 7,
        compiler_params=pltpu.CompilerParams(vmem_limit_bytes=32 * 1024 * 1024),
    )(reset, field, fin_a, fin_r, bias, q5, rows_out)
    back = lambda v: v.transpose(3, 0, 1, 2)
    return back(h_new), back(grad_x), back(grad_h), wgg, gb, wgc, cb.reshape(32)


def solution(mesh):
    field = P("filt", None, None, "wedge")
    in_specs = (
        field, field, P(), P(None, None, None, "filt", None, None), P(None, "filt"),
        P(None, None, None, "filt", None), P("filt"), field,
    )
    out_specs = (
        field, field, field, P(None, None, None, "filt", None, None), P(None, "filt"),
        P(None, None, None, "filt", None), P("filt"),
    )
    return jax.shard_map(per_device, mesh=mesh, in_specs=in_specs, out_specs=out_specs, check_vma=False)
```

```python
import numpy as np
import jax
import jax.numpy as jnp
from jax import lax
from jax.experimental import pallas as pl
from jax.experimental.pallas import tpu as pltpu
from jax.sharding import PartitionSpec as P

XN, ZH, YN, ZL, CN = 4, 2, 4, 8, 2
WEDGES = YN * ZL * CN
COPIES = 112
MESH = pl.DeviceIdType.MESH
BF = jnp.bfloat16
F32 = jnp.float32
NT = (((1,), (1,)), ((), ()))


def block_transpose(first, second, third):
    size = first * second * third
    order = np.arange(size).reshape(first, second, third).transpose(1, 0, 2).reshape(-1)
    matrix = np.zeros((size, size), np.float32)
    matrix[order, np.arange(size)] = 1.0
    return matrix


def row_order():
    order = np.arange(128).reshape(8, 16).T.reshape(-1)
    matrix = np.zeros((128, 128), np.float32)
    matrix[np.arange(128), order] = 1.0
    return matrix


def roll(v, shift):
    return pltpu.roll(v, shift, 1)


def slot_a(shape):
    return lax.broadcasted_iota(jnp.int32, shape, 1) % 64 < 32


def swap(v):
    return jnp.where(slot_a(v.shape), roll(v, 96), roll(v, 32))


def dot(a, b):
    return jnp.dot(a, b, preferred_element_type=F32)


def dot_nt(a, b):
    return lax.dot_general(a, b, NT, preferred_element_type=F32)


def tiles(ref):
    return jnp.concatenate([ref[t] for t in range(4)], axis=1)


def taps(ref, start, rows):
    return jnp.concatenate([ref[start + e * 8:start + e * 8 + rows, :].astype(BF) for e in range(3)], axis=1)


def shifted(v, start, rows):
    out = None
    for e in range(3):
        part = v[start + (2 - e) * 8:start + (2 - e) * 8 + rows, e * 128:e * 128 + 128]
        out = part if out is None else out + part
    return out


def kernel(
    reset_ref, x_ref, h_ref, ct_ref, wg_ref, wc_ref, gb_ref, cb_ref, q5_ref, pm_ref,
    field_ref, fin_a, fin_r, bias_ref,
    f_ref, halo_l, halo_r, uf, near_l, near_r, far, hp, cp, wq, wch, w_upd, w_res, w_cx, w_ch,
    bz_s, bz_r, gs_ri, gr_ri, gs_ui, gr_ui, gs_re, gr_re, gs_ue, gr_ue,
    zs_ri, zr_ri, zs_ui, zr_ui, zs_re, zr_re, zs_ue, zr_ue, gpf, cs, cr,
    g1c, g1u, g2, ut, vt, blob_a, blob_r, core_a, mid_a, y_a, m_r,
    zs_a, zq_a, zf_a, zs_b, zq_b, zf_b, bs, br, bs2, br2,
    send_sems, recv_sems, up_s, up_r, down_s, down_r,
):
    w = lax.axis_index("wedge")
    f = lax.axis_index("filt")
    x, zh = f // ZH, f % ZH
    core, zl, yy = w % CN, (w // CN) % ZL, w // (CN * ZL)
    m = yy * CN + core
    first_z = zh == 0
    fp = x * ZH + (1 - zh)
    after, before = (w + 1) % WEDGES, (w + WEDGES - 1) % WEDGES

    def xpeer(d):
        return (w, ((x + d) % XN) * ZH + zh)

    def at_y(t, c):
        return (t * ZL + zl) * CN + c, f

    def mpeer(d):
        t = (m + d) % 8
        return at_y(t // CN, t % CN)

    def ypeer(d):
        return at_y((yy + d) % YN, core)

    def lpeer(d):
        return (yy * ZL + (zl + d + ZL) % ZL) * CN + core, f

    partner = (w, fp)
    other_core = at_y(yy, 1 - core)
    peers = [(after, f), (before, f), (after, fp), (before, fp), partner] + [xpeer(d) for d in (1, 2, 3)]
    peers += [mpeer(d) for d in range(1, 8)] + [lpeer(d) for d in range(1, 8)]
    barrier = pltpu.get_barrier_semaphore()
    for peer in peers:
        pl.semaphore_signal(barrier, inc=1, device_id=peer, device_id_type=MESH)

    def own_a(v):
        return jnp.where(first_z, v, swap(v))

    def own_b(v):
        return jnp.where(first_z, swap(v), v)

    order = pm_ref[...]
    kept = jnp.concatenate(
        [h_ref[b:b + 1].astype(F32) * (1 - reset_ref[b]).astype(F32) for b in range(8)], axis=0
    )
    near, wide = [], []
    for i in range(2):
        hidden = kept[:, i].reshape(128, 32)
        near += [x_ref[:, i].reshape(128, 32).astype(F32), hidden]
        wide += [ct_ref[:, i].reshape(128, 32).astype(F32), hidden]
    own_u = dot(order, jnp.concatenate(near, axis=1).astype(BF))
    own_c = dot(order, jnp.concatenate(wide, axis=1).astype(BF))
    f_ref[:, :128] = own_u.astype(BF)
    f_ref[:, 128:] = own_c.astype(BF)
    uf[32:160, :] = own_u
    row = lax.broadcasted_iota(jnp.int32, (8, 128), 0)
    bias_rows = [jnp.concatenate([v] * 4, axis=1) for v in (gb_ref[0:1, :], gb_ref[1:2, :], cb_ref[...])]
    bias_rows = jnp.where(row == 0, bias_rows[0], jnp.where(row == 1, bias_rows[1], bias_rows[2]))
    bz_s[...] = jnp.where(slot_a((8, 128)) == first_z, bias_rows, 0.0)
    q5 = q5_ref[...]

    def arrange(nat, out_ref):
        lhs = jnp.concatenate(
            [
                jnp.concatenate([nat(a, e) for a in (ip + 1, ip)], axis=1)
                for e in range(3)
                for ip in range(2)
            ],
            axis=0,
        )
        out = dot_nt(lhs, q5).astype(BF)
        for t in range(4):
            out_ref[t] = out[:, t * 128:t * 128 + 128]

    def both(gate):
        def nat(a, e):
            return jnp.concatenate([wg_ref[((s * 3 + a) * 3 + e) * 32:((s * 3 + a) * 3 + e) * 32 + 32, gate * 256:gate * 256 + 256] for s in range(2)], axis=0)

        return nat

    def input_only(a, e):
        at = (a * 3 + e) * 32
        return jnp.concatenate([wc_ref[at:at + 32, :], jnp.zeros((32, 256), BF)], axis=0)

    def pair_hidden(a, e):
        at = (a * 3 + e) * 32
        return jnp.concatenate([wch[0, at:at + 32, :], wch[1, at:at + 32, :]], axis=0)

    arrange(both(1), w_res)
    arrange(both(0), w_upd)
    arrange(input_only, w_cx)
    pl.semaphore_wait(barrier, len(peers))

    sends = []

    def push(src, dst, peer):
        at = len(sends)
        copy = pltpu.make_async_remote_copy(
            src_ref=src, dst_ref=dst, send_sem=send_sems.at[at], recv_sem=recv_sems.at[at],
            device_id=peer, device_id_type=MESH,
        )
        copy.start()
        sends.append(copy)
        return copy

    def landed(copies):
        for copy in copies:
            copy.wait_recv()

    right, left = pl.ds(96, 32), pl.ds(0, 32)
    second = pl.ds(128, 128)
    halo = [
        push(f_ref.at[right, :], halo_l, (after, f)),
        push(f_ref.at[left, :], halo_r, (before, f)),
    ]
    pair = [
        push(f_ref.at[right, second], near_l, (after, fp)),
        push(f_ref.at[left, second], near_r, (before, fp)),
        push(f_ref.at[:, second], far, partner),
        push(bz_s, bz_r, partner),
    ]
    part = pl.multiple_of(288 + (m % 6) * 48, 16)
    pair_w = push(wc_ref.at[pl.ds(part, 48), :], wq.at[m], partner)
    def partial(lhs, gs_r, gr_r, gs_u, gr_u):
        res, upd = [], []
        for d in (2, 1, 3, 0):
            t = (x + d) % XN
            gs_r[t] = dot(lhs, w_res[t]).astype(BF)
            if d:
                res.append(push(gs_r.at[t], gr_r.at[d - 1], xpeer(d)))
        for d in (2, 1, 3, 0):
            t = (x + d) % XN
            gs_u[t] = dot(lhs, jnp.concatenate([w_upd[t], w_cx[t]], axis=1)).astype(BF)
            if d:
                upd.append(push(gs_u.at[t], gr_u.at[d - 1], xpeer(d)))
        return res, upd

    def summed(gs, gr, copies, zs, zr):
        value = gs[x].astype(F32)
        landed(copies)
        for d in range(3):
            value = value + gr[d].astype(F32)
        zs[...] = value.astype(BF)
        return value, push(zs, zr, partner)

    res_i, upd_i = partial(taps(uf, 32, 112), gs_ri, gr_ri, gs_ui, gr_ui)
    sum_ri, zri = summed(gs_ri, gr_ri, res_i, zs_ri, zr_ri)
    landed(halo)
    uf[0:32, :] = halo_l[:, :128].astype(F32)
    uf[160:192, :] = halo_r[:, :128].astype(F32)
    lhs = jnp.concatenate([taps(uf, 0, 32), taps(uf, 144, 32)], axis=0)
    res_e, upd_e = partial(lhs, gs_re, gr_re, gs_ue, gr_ue)
    sum_re, zre = summed(gs_re, gr_re, res_e, zs_re, zr_re)
    sum_ui, zui = summed(gs_ui, gr_ui, upd_i, zs_ui, zr_ui)
    sum_ue, zue = summed(gs_ue, gr_ue, upd_e, zs_ue, zr_ue)
    pair_w.wait_recv()
    shares = [push(wq.at[m], wq.at[m], mpeer(d)) for d in range(1, 8)]

    for e in range(3):
        ut[e * 128:e * 128 + 128, :] = uf[(e + 3) * 8:(e + 3) * 8 + 128, :].T.astype(BF)
    landed(pair)
    biases = bz_s[...] + bz_r[...]
    for lo, mine, theirs in (
        (0, halo_l[:, 128:], near_l[...]), (32, f_ref[:, 128:], far[...]), (160, halo_r[:, 128:], near_r[...])
    ):
        mine, theirs = mine.astype(F32), theirs.astype(F32)
        block_0 = jnp.where(first_z, mine, theirs)
        block_1 = jnp.where(first_z, theirs, mine)
        at = slot_a(mine.shape)
        hp[lo:lo + mine.shape[0], :] = jnp.where(at, swap(block_0), block_1)
        cp[lo:lo + mine.shape[0], :] = jnp.where(at, block_0, swap(block_1))
    landed(shares)
    wch[zh] = wc_ref[288:576, :]
    for k in range(6):
        wch[1 - zh, k * 48:k * 48 + 48, :] = wq[k]
    arrange(pair_hidden, w_ch)

    def joined(edge, inner):
        return jnp.concatenate([edge[:32], inner, edge[32:]], axis=0)

    landed([zri, zre])
    sum_r = joined(sum_re + zr_re[...].astype(F32), sum_ri + zr_ri[...].astype(F32))
    r = jax.nn.sigmoid(sum_r + biases[1:2, :])
    gp = (r * hp[8:184, :]).astype(BF).astype(F32)
    gpf[...] = gp

    lhs = taps(gpf, 0, 160)
    cand = []
    for d in (2, 1, 3, 0):
        t = (x + d) % XN
        cs[t] = dot(lhs, w_ch[t]).astype(BF)
        if d:
            cand.append(push(cs.at[t], cr.at[d - 1], xpeer(d)))
    own_v = jnp.where(slot_a((176, 128)), uf[8:184, :], own_b(gp))
    for e in range(3):
        vt[e * 128:e * 128 + 128, :] = own_v[(e + 2) * 8:(e + 2) * 8 + 128].T.astype(BF)
    landed([zui, zue])
    sum_u = joined(sum_ue + zr_ue[...].astype(F32), sum_ui + zr_ui[...].astype(F32))[8:168]
    u = jax.nn.sigmoid(sum_u[:, :128] + biases[0:1, :])
    pre = sum_u[:, 128:] + biases[2:3, :] + cs[x].astype(F32)
    landed(cand)
    for d in range(3):
        pre = pre + cr[d].astype(F32)
    fresh = jnp.tanh(pre)
    h = hp[16:176, :]
    cot = cp[16:176, :]
    cg = (cot * u * (1.0 - fresh * fresh)).astype(BF)
    g1c[x] = cg
    got_c = [push(g1c.at[x], g1c.at[x], xpeer(d)) for d in (2, 1, 3)]
    ug = (cot * (fresh - h) * u * (1.0 - u)).astype(BF)
    g1u[x] = ug
    got_u = [push(g1u.at[x], g1u.at[x], xpeer(d)) for d in (2, 1, 3)]
    direct = (cot * (1.0 - u))[16:144]
    hn = ((1.0 - u) * h + u * fresh)[16:144]
    field_ref[:, :128] = own_a(hn).astype(BF)
    sum_c = jnp.sum(cg[16:144].astype(F32), axis=0, keepdims=True)
    sum_g = jnp.sum(ug[16:144].astype(F32), axis=0, keepdims=True)

    landed(got_c)
    grads = tiles(g1c)
    gg = shifted(dot_nt(grads, tiles(w_ch)), 0, 144)
    r_near = r[16:160]
    rt = (gg * hp[24:168, :] * r_near * (1.0 - r_near)).astype(BF).astype(F32)
    edge = jnp.zeros((8, 128), F32)
    g2[x] = jnp.concatenate([edge, rt, edge], axis=0).astype(BF)
    got_r = [push(g2.at[x], g2.at[x], xpeer(d)) for d in (2, 1, 3)]
    sum_q = jnp.sum(rt[8:136], axis=0, keepdims=True)
    bs[...] = jnp.where(row == 0, sum_g, jnp.where(row == 1, sum_q, jnp.where(row == 2, sum_c, 0.0)))
    bias1 = [push(bs, br.at[d - 1], mpeer(d)) for d in range(1, 8)]

    low = lax.broadcasted_iota(jnp.int32, (64, 128), 1) < 64

    def weight_grad(left_ref, grad_ref, place):
        left_rows = left_ref[...]
        for q in range(2):
            rhs = jnp.concatenate([grad_ref[2 * q, 16:144, :], grad_ref[2 * q + 1, 16:144, :]], axis=1)
            product = dot(left_rows, rhs)
            for e in range(3):
                t0 = product[e * 128:e * 128 + 128, :128]
                t1 = product[e * 128:e * 128 + 128, 128:]
                slabs = (
                    jnp.where(low, t0[64:], t0[:64]),
                    jnp.where(low, t1[64:], t1[:64]),
                    jnp.where(low, t0[:64] + roll(t0[64:], 64), t1[64:] + roll(t1[:64], 64)),
                )
                for k, slab in enumerate(slabs):
                    out_ref, n = place(e, q * 3 + k)
                    out_ref[n * 64:n * 64 + 64, :] = slab.astype(BF)

    def chunk(t, rows):
        return pl.ds(pl.multiple_of(t * rows, 16), rows)

    weight_grad(vt, g1c, lambda e, k: (blob_a, e * 6 + k))
    landed(got_u)
    weight_grad(ut, g1u, lambda e, k: (blob_a, 18 + e * 6 + k) if e < 2 else (blob_r, 18 + k))
    half = [push(blob_a.at[chunk(t * CN + 1 - core, 240), :], core_a.at[t], other_core) for t in range(4)]
    total = shifted(dot_nt(grads, tiles(w_cx)), 8, 128) + shifted(dot_nt(tiles(g1u), tiles(w_upd)), 8, 128)
    landed(got_r)
    weight_grad(ut, g2, lambda e, k: (blob_r, e * 6 + k))
    over_m = [push(blob_r.at[chunk((m + d) % 8, 192), :], m_r.at[d - 1], mpeer(d)) for d in range(1, 8)]
    landed(half)
    for t in range(4):
        mid_a[t] = (blob_a[chunk(t * CN + core, 240), :].astype(F32) + core_a[t].astype(F32)).astype(BF)
    over_y = [push(mid_a.at[(yy + d) % YN], y_a.at[d - 1], ypeer(d)) for d in (2, 1, 3)]
    total = total + shifted(dot_nt(tiles(g2), tiles(w_res)), 8, 128)
    hidden = own_b(direct + gg[8:136] * r[24:152])
    field_ref[:, 128:] = jnp.where(slot_a((128, 128)), total, hidden + total).astype(BF)

    def reduce_z(owners, mine, came, out, which):
        def copy(src, dst, send, recv, z):
            return pltpu.make_async_remote_copy(
                src_ref=src, dst_ref=dst, send_sem=send, recv_sem=recv, device_id=lpeer(z - zl), device_id_type=MESH
            )

        def up(i, s, p):
            return copy(mine.at[i], came.at[s], up_s.at[which, i], up_r.at[which, s], p)

        def down(i, d, z):
            return copy(out.at[i], out.at[i], down_s.at[which, d - 1], down_r.at[which, i], z)

        for i, p in enumerate(owners):
            pl.when(zl != p)(up(i, zl, p).start)

        def own():
            for i, p in enumerate(owners):
                @pl.when(zl == p)
                def _():
                    value = mine[i].astype(F32)
                    for s in range(8):
                        if s != p:
                            up(i, s, p).wait_recv()
                            value = value + came[s].astype(F32)
                    out[i] = value.astype(BF)
                    for d in range(1, 8):
                        down(i, d, (p + d) % 8).start()

        def back():
            for i, p in enumerate(owners):
                pl.when(zl != p)(down(i, 1, p).wait_recv)

        def close():
            for i, p in enumerate(owners):
                @pl.when(zl != p)
                def _():
                    up(i, zl, p).wait_send()

                @pl.when(zl == p)
                def _():
                    for d in range(1, 8):
                        down(i, d, (p + d) % 8).wait_send()

        return own, back, close

    acc = mid_a[yy].astype(F32)
    landed(over_y)
    for d in range(3):
        acc = acc + y_a[d].astype(F32)
    for p in range(3):
        zs_a[p] = acc[p * 80:p * 80 + 80].astype(BF)
    own_za, back_za, close_za = reduce_z((2, 3, 4), zs_a, zq_a, zf_a, 0)
    b1 = bs[...]
    landed(bias1)
    for d in range(7):
        b1 = b1 + br[d]
    bs2[...] = b1
    bias2 = [push(bs2, br2.at[d - 1], lpeer(d)) for d in range(1, 8)]
    acc = blob_r[chunk(m, 192), :].astype(F32)
    landed(over_m)
    for d in range(7):
        acc = acc + m_r[d].astype(F32)
    for p in range(2):
        zs_b[p] = acc[p * 96:p * 96 + 96].astype(BF)
    own_zb, back_zb, close_zb = reduce_z((3, 4), zs_b, zq_b, zf_b, 1)
    own_za()
    own_zb()

    def spread(fin):
        to_y = [push(fin.at[m], fin.at[m], ypeer(d)) for d in (2, 1, 3)]
        return to_y, [push(fin.at[m], fin.at[m], other_core)]

    def forward(fin, to_y, rest):
        for copy, d in zip(to_y, (2, 1, 3)):
            copy.wait_recv()
            at = ((yy + YN - d) % YN) * CN + core
            rest.append(push(fin.at[at], fin.at[at], other_core))

    back_za()
    for p in range(3):
        fin_a[m, p * 80:p * 80 + 80, :] = zf_a[p]
    to_ya, rest_a = spread(fin_a)
    back_zb()
    for p in range(2):
        fin_r[m, p * 96:p * 96 + 96, :] = zf_b[p]
    to_yr, rest_r = spread(fin_r)
    b2 = bs2[...]
    landed(bias2)
    for d in range(7):
        b2 = b2 + br2[d]
    bias_ref[...] = own_a(b2)
    forward(fin_r, to_yr, rest_r)
    forward(fin_a, to_ya, rest_a)
    landed(rest_a)
    landed(rest_r)
    close_za()
    close_zb()
    for copy in sends:
        copy.wait_send()


def finish(
    reset_ref, field_ref, fin_a, fin_r, bias_ref, q5_ref, pm_ref,
    hn_ref, gx_ref, gh_ref, wgg_ref, gb_ref, wgc_ref, cb_ref,
):
    rows = dot(pm_ref[...], field_ref[...])
    for i in range(2):
        hn_ref[:, i] = rows[:, i * 64:i * 64 + 32].reshape(8, 16, 32).astype(BF)
        gx_ref[:, i] = rows[:, 128 + i * 64:160 + i * 64].reshape(8, 16, 32).astype(BF)
        value = rows[:, 160 + i * 64:192 + i * 64].reshape(8, 16, 32)
        for b in range(8):
            gh_ref[b, i] = (value[b] * (1 - reset_ref[b]).astype(F32)).astype(BF)
    sums = bias_ref[...]
    sums = sums + roll(sums, 64)
    gb_ref[...] = sums[0:2, 0:32]
    cb_ref[...] = sums[2:3, 0:32]

    def slab_a(n):
        pieces = [fin_a[r // 240, r % 240:r % 240 + 16, :] for r in range(n * 64, n * 64 + 64, 16)]
        return jnp.concatenate(pieces, axis=0)

    def slab_r(n):
        return fin_r[n // 3, n % 3 * 64:n % 3 * 64 + 64, :]

    def put(gate, a, e, value):
        for s in range(2):
            part = value[s * 32:s * 32 + 32]
            if gate is None:
                wgc_ref[s, a, e] = part
            else:
                wgg_ref[s, a, e, :, gate, :] = part

    q5 = q5_ref[...]
    for gate in (None, 0, 1):
        def get(e, q, k):
            n = e * 6 + q * 3 + k
            if gate is None:
                return slab_a(n)
            if gate == 1:
                return slab_r(n)
            return slab_a(18 + n) if e < 2 else slab_r(6 + n)

        outer = jnp.concatenate(
            [
                jnp.concatenate([get(e, q, k) for q in range(2) for k in range(2)], axis=1)
                for e in range(3)
            ],
            axis=0,
        )
        outer = dot(outer, q5)
        for e in range(3):
            at = slice(e * 64, e * 64 + 64)
            put(gate, 2, e, outer[at, :256])
            put(gate, 0, e, outer[at, 256:])
            inner = jnp.concatenate([get(e, q, 2) for q in range(2)], axis=1)
            put(gate, 1, e, inner.astype(F32))


def per_device(x_in, h_prev, reset, w_gate, gate_bias, w_cand, cand_bias, cotangent):
    def bf(*shape):
        return pltpu.VMEM(shape, BF)

    def f32(*shape):
        return pltpu.VMEM(shape, F32)

    scratch = [
        bf(128, 256), bf(32, 256), bf(32, 256), f32(192, 128), bf(32, 128), bf(32, 128), bf(128, 128),
        f32(192, 128), f32(192, 128), bf(8, 48, 256), bf(2, 288, 256),
        bf(4, 384, 128), bf(4, 384, 128), bf(4, 384, 128), bf(4, 384, 128),
        f32(8, 128), f32(8, 128), bf(4, 112, 128), bf(3, 112, 128), bf(4, 112, 256), bf(3, 112, 256),
        bf(4, 64, 128), bf(3, 64, 128), bf(4, 64, 256), bf(3, 64, 256),
        bf(112, 128), bf(112, 128), bf(112, 256), bf(112, 256), bf(64, 128), bf(64, 128), bf(64, 256), bf(64, 256),
        f32(176, 128), bf(4, 160, 128), bf(3, 160, 128),
        bf(4, 160, 128), bf(4, 160, 128), bf(4, 160, 128), bf(384, 128), bf(384, 128),
        bf(1920, 128), bf(1536, 128), bf(4, 240, 128), bf(4, 240, 128), bf(3, 240, 128), bf(7, 192, 128),
        bf(3, 80, 128), bf(8, 80, 128), bf(3, 80, 128), bf(2, 96, 128), bf(8, 96, 128), bf(2, 96, 128),
        f32(8, 128), f32(7, 8, 128), f32(8, 128), f32(7, 8, 128),
        pltpu.SemaphoreType.DMA((COPIES,)), pltpu.SemaphoreType.DMA((COPIES,)),
        pltpu.SemaphoreType.DMA((2, 4)), pltpu.SemaphoreType.DMA((2, 8)),
        pltpu.SemaphoreType.DMA((2, 7)), pltpu.SemaphoreType.DMA((2, 4)),
    ]
    q5 = jnp.asarray(block_transpose(4, 2, 64), BF)
    rows_in = jnp.asarray(row_order(), BF)
    rows_out = jnp.asarray(row_order().T, BF)
    near = lambda v: v.transpose(1, 2, 3, 0)
    smem = pl.BlockSpec(memory_space=pltpu.SMEM)
    whole = pl.BlockSpec(memory_space=pltpu.VMEM)
    field, fin_a, fin_r, bias = pl.pallas_call(
        kernel,
        out_shape=(
            jax.ShapeDtypeStruct((128, 256), BF),
            jax.ShapeDtypeStruct((8, 240, 128), BF),
            jax.ShapeDtypeStruct((8, 192, 128), BF),
            jax.ShapeDtypeStruct((8, 128), F32),
        ),
        in_specs=[smem] + [whole] * 9,
        out_specs=[whole] * 4,
        scratch_shapes=scratch,
        compiler_params=pltpu.CompilerParams(
            collective_id=0, has_side_effects=True, vmem_limit_bytes=48 * 1024 * 1024
        ),
        cost_estimate=pl.CostEstimate(flops=1_000_000_000, bytes_accessed=8_000_000, transcendentals=100_000),
    )(
        reset, near(x_in), near(h_prev), near(cotangent), w_gate.reshape(576, 512), w_cand.reshape(576, 256),
        gate_bias, cand_bias.reshape(1, 32), q5, rows_in,
    )
    shape = jax.ShapeDtypeStruct((8, 2, 16, 32), BF)
    h_new, grad_x, grad_h, wgg, gb, wgc, cb = pl.pallas_call(
        finish,
        out_shape=(
            shape, shape, shape,
            jax.ShapeDtypeStruct(w_gate.shape, F32), jax.ShapeDtypeStruct((2, 32), F32),
            jax.ShapeDtypeStruct(w_cand.shape, F32), jax.ShapeDtypeStruct((1, 32), F32),
        ),
        in_specs=[smem] + [whole] * 6,
        out_specs=[whole] * 7,
        compiler_params=pltpu.CompilerParams(vmem_limit_bytes=32 * 1024 * 1024),
    )(reset, field, fin_a, fin_r, bias, q5, rows_out)
    back = lambda v: v.transpose(3, 0, 1, 2)
    return back(h_new), back(grad_x), back(grad_h), wgg, gb, wgc, cb.reshape(32)


def solution(mesh):
    field = P("filt", None, None, "wedge")
    in_specs = (
        field, field, P(), P(None, None, None, "filt", None, None), P(None, "filt"),
        P(None, None, None, "filt", None), P("filt"), field,
    )
    out_specs = (
        field, field, field, P(None, None, None, "filt", None, None), P(None, "filt"),
        P(None, None, None, "filt", None), P("filt"),
    )
    return jax.shard_map(per_device, mesh=mesh, in_specs=in_specs, out_specs=out_specs, check_vma=False)
```

```python
import numpy as np
import jax
import jax.numpy as jnp
from jax import lax
from jax.experimental import pallas as pl
from jax.experimental.pallas import tpu as pltpu
from jax.sharding import PartitionSpec as P

XN, ZH, YN, ZL, CN = 4, 2, 4, 8, 2
WEDGES = YN * ZL * CN
COPIES = 112
MESH = pl.DeviceIdType.MESH
BF = jnp.bfloat16
F32 = jnp.float32
NT = (((1,), (1,)), ((), ()))


def block_transpose(first, second, third):
    size = first * second * third
    order = np.arange(size).reshape(first, second, third).transpose(1, 0, 2).reshape(-1)
    matrix = np.zeros((size, size), np.float32)
    matrix[order, np.arange(size)] = 1.0
    return matrix


def row_order():
    order = np.arange(128).reshape(8, 16).T.reshape(-1)
    matrix = np.zeros((128, 128), np.float32)
    matrix[np.arange(128), order] = 1.0
    return matrix


def roll(v, shift):
    return pltpu.roll(v, shift, 1)


def slot_a(shape):
    return lax.broadcasted_iota(jnp.int32, shape, 1) % 64 < 32


def swap(v):
    return jnp.where(slot_a(v.shape), roll(v, 96), roll(v, 32))


def dot(a, b):
    return jnp.dot(a, b, preferred_element_type=F32)


def dot_nt(a, b):
    return lax.dot_general(a, b, NT, preferred_element_type=F32)


def tiles(ref):
    return jnp.concatenate([ref[t] for t in range(4)], axis=1)


def taps(ref, start, rows):
    return jnp.concatenate([ref[start + e * 8:start + e * 8 + rows, :].astype(BF) for e in range(3)], axis=1)


def shifted(v, start, rows):
    out = None
    for e in range(3):
        part = v[start + (2 - e) * 8:start + (2 - e) * 8 + rows, e * 128:e * 128 + 128]
        out = part if out is None else out + part
    return out


def kernel(
    reset_ref, x_ref, h_ref, ct_ref, wg_ref, wc_ref, gb_ref, cb_ref, q5_ref, pm_ref,
    field_ref, fin_a, fin_r, bias_ref,
    f_ref, halo_l, halo_r, uf, near_l, near_r, far, hp, cp, wq, wch, w_upd, w_res, w_cx, w_ch,
    bz_s, bz_r, gs_ri, gr_ri, gs_ui, gr_ui, gs_re, gr_re, gs_ue, gr_ue,
    zs_ri, zr_ri, zs_ui, zr_ui, zs_re, zr_re, zs_ue, zr_ue, gpf, cs, cr,
    g1c, g1u, g2, ut, vt, blob_a, blob_r, core_a, mid_a, y_a, m_r,
    zs_a, zq_a, zf_a, zs_b, zq_b, zf_b, bs, br, bs2, br2,
    send_sems, recv_sems, up_s, up_r, down_s, down_r,
):
    w = lax.axis_index("wedge")
    f = lax.axis_index("filt")
    x, zh = f // ZH, f % ZH
    core, zl, yy = w % CN, (w // CN) % ZL, w // (CN * ZL)
    m = yy * CN + core
    first_z = zh == 0
    fp = x * ZH + (1 - zh)
    after, before = (w + 1) % WEDGES, (w + WEDGES - 1) % WEDGES

    def xpeer(d):
        return (w, ((x + d) % XN) * ZH + zh)

    def at_y(t, c):
        return (t * ZL + zl) * CN + c, f

    def mpeer(d):
        t = (m + d) % 8
        return at_y(t // CN, t % CN)

    def ypeer(d):
        return at_y((yy + d) % YN, core)

    def lpeer(d):
        return (yy * ZL + (zl + d + ZL) % ZL) * CN + core, f

    partner = (w, fp)
    other_core = at_y(yy, 1 - core)
    peers = [(after, f), (before, f), (after, fp), (before, fp), partner] + [xpeer(d) for d in (1, 2, 3)]
    peers += [mpeer(d) for d in range(1, 8)] + [lpeer(d) for d in range(1, 8)]
    barrier = pltpu.get_barrier_semaphore()
    for peer in peers:
        pl.semaphore_signal(barrier, inc=1, device_id=peer, device_id_type=MESH)

    def own_a(v):
        return jnp.where(first_z, v, swap(v))

    def own_b(v):
        return jnp.where(first_z, swap(v), v)

    order = pm_ref[...]
    kept = jnp.concatenate(
        [h_ref[b:b + 1].astype(F32) * (1 - reset_ref[b]).astype(F32) for b in range(8)], axis=0
    )
    near, wide = [], []
    for i in range(2):
        hidden = kept[:, i].reshape(128, 32)
        near += [x_ref[:, i].reshape(128, 32).astype(F32), hidden]
        wide += [ct_ref[:, i].reshape(128, 32).astype(F32), hidden]
    own_u = dot(order, jnp.concatenate(near, axis=1).astype(BF))
    own_c = dot(order, jnp.concatenate(wide, axis=1).astype(BF))
    f_ref[:, :128] = own_u.astype(BF)
    f_ref[:, 128:] = own_c.astype(BF)
    uf[32:160, :] = own_u
    row = lax.broadcasted_iota(jnp.int32, (8, 128), 0)
    bias_rows = [jnp.concatenate([v] * 4, axis=1) for v in (gb_ref[0:1, :], gb_ref[1:2, :], cb_ref[...])]
    bias_rows = jnp.where(row == 0, bias_rows[0], jnp.where(row == 1, bias_rows[1], bias_rows[2]))
    bz_s[...] = jnp.where(slot_a((8, 128)) == first_z, bias_rows, 0.0)
    q5 = q5_ref[...]

    def arrange(nat, out_ref):
        lhs = jnp.concatenate(
            [
                jnp.concatenate([nat(a, e) for a in (ip + 1, ip)], axis=1)
                for e in range(3)
                for ip in range(2)
            ],
            axis=0,
        )
        out = dot_nt(lhs, q5).astype(BF)
        for t in range(4):
            out_ref[t] = out[:, t * 128:t * 128 + 128]

    def both(gate):
        def nat(a, e):
            return jnp.concatenate([wg_ref[((s * 3 + a) * 3 + e) * 32:((s * 3 + a) * 3 + e) * 32 + 32, gate * 256:gate * 256 + 256] for s in range(2)], axis=0)

        return nat

    def input_only(a, e):
        at = (a * 3 + e) * 32
        return jnp.concatenate([wc_ref[at:at + 32, :], jnp.zeros((32, 256), BF)], axis=0)

    def pair_hidden(a, e):
        at = (a * 3 + e) * 32
        return jnp.concatenate([wch[0, at:at + 32, :], wch[1, at:at + 32, :]], axis=0)

    arrange(both(1), w_res)
    arrange(both(0), w_upd)
    arrange(input_only, w_cx)
    pl.semaphore_wait(barrier, len(peers))

    sends = []

    def push(src, dst, peer):
        at = len(sends)
        copy = pltpu.make_async_remote_copy(
            src_ref=src, dst_ref=dst, send_sem=send_sems.at[at], recv_sem=recv_sems.at[at],
            device_id=peer, device_id_type=MESH,
        )
        copy.start()
        sends.append(copy)
        return copy

    def landed(copies):
        for copy in copies:
            copy.wait_recv()

    right, left = pl.ds(96, 32), pl.ds(0, 32)
    second = pl.ds(128, 128)
    halo = [
        push(f_ref.at[right, :], halo_l, (after, f)),
        push(f_ref.at[left, :], halo_r, (before, f)),
    ]
    pair = [
        push(f_ref.at[right, second], near_l, (after, fp)),
        push(f_ref.at[left, second], near_r, (before, fp)),
        push(f_ref.at[:, second], far, partner),
        push(bz_s, bz_r, partner),
    ]
    part = pl.multiple_of(288 + (m % 6) * 48, 16)
    pair_w = push(wc_ref.at[pl.ds(part, 48), :], wq.at[m], partner)
    def partial(lhs, gs_r, gr_r, gs_u, gr_u):
        res, upd = [], []
        for d in (2, 1, 3, 0):
            t = (x + d) % XN
            gs_r[t] = dot(lhs, w_res[t]).astype(BF)
            if d:
                res.append(push(gs_r.at[t], gr_r.at[d - 1], xpeer(d)))
        for d in (2, 1, 3, 0):
            t = (x + d) % XN
            gs_u[t] = dot(lhs, jnp.concatenate([w_upd[t], w_cx[t]], axis=1)).astype(BF)
            if d:
                upd.append(push(gs_u.at[t], gr_u.at[d - 1], xpeer(d)))
        return res, upd

    def summed(gs, gr, copies, zs, zr):
        value = gs[x].astype(F32)
        landed(copies)
        for d in range(3):
            value = value + gr[d].astype(F32)
        zs[...] = value.astype(BF)
        return value, push(zs, zr, partner)

    res_i, upd_i = partial(taps(uf, 32, 112), gs_ri, gr_ri, gs_ui, gr_ui)
    sum_ri, zri = summed(gs_ri, gr_ri, res_i, zs_ri, zr_ri)
    landed(halo)
    uf[0:32, :] = halo_l[:, :128].astype(F32)
    uf[160:192, :] = halo_r[:, :128].astype(F32)
    lhs = jnp.concatenate([taps(uf, 0, 32), taps(uf, 144, 32)], axis=0)
    res_e, upd_e = partial(lhs, gs_re, gr_re, gs_ue, gr_ue)
    sum_re, zre = summed(gs_re, gr_re, res_e, zs_re, zr_re)
    sum_ui, zui = summed(gs_ui, gr_ui, upd_i, zs_ui, zr_ui)
    sum_ue, zue = summed(gs_ue, gr_ue, upd_e, zs_ue, zr_ue)
    pair_w.wait_recv()
    shares = [push(wq.at[m], wq.at[m], mpeer(d)) for d in range(1, 8)]

    for e in range(3):
        ut[e * 128:e * 128 + 128, :] = uf[(e + 3) * 8:(e + 3) * 8 + 128, :].T.astype(BF)
    landed(pair)
    biases = bz_s[...] + bz_r[...]
    for lo, mine, theirs in (
        (0, halo_l[:, 128:], near_l[...]), (32, f_ref[:, 128:], far[...]), (160, halo_r[:, 128:], near_r[...])
    ):
        mine, theirs = mine.astype(F32), theirs.astype(F32)
        block_0 = jnp.where(first_z, mine, theirs)
        block_1 = jnp.where(first_z, theirs, mine)
        at = slot_a(mine.shape)
        hp[lo:lo + mine.shape[0], :] = jnp.where(at, swap(block_0), block_1)
        cp[lo:lo + mine.shape[0], :] = jnp.where(at, block_0, swap(block_1))
    landed(shares)
    wch[zh] = wc_ref[288:576, :]
    for k in range(6):
        wch[1 - zh, k * 48:k * 48 + 48, :] = wq[k]
    arrange(pair_hidden, w_ch)

    def joined(edge, inner):
        return jnp.concatenate([edge[:32], inner, edge[32:]], axis=0)

    landed([zri, zre])
    sum_r = joined(sum_re + zr_re[...].astype(F32), sum_ri + zr_ri[...].astype(F32))
    r = jax.nn.sigmoid(sum_r + biases[1:2, :])
    gp = (r * hp[8:184, :]).astype(BF).astype(F32)
    gpf[...] = gp

    lhs = taps(gpf, 0, 160)
    cand = []
    for d in (2, 1, 3, 0):
        t = (x + d) % XN
        cs[t] = dot(lhs, w_ch[t]).astype(BF)
        if d:
            cand.append(push(cs.at[t], cr.at[d - 1], xpeer(d)))
    own_v = jnp.where(slot_a((176, 128)), uf[8:184, :], own_b(gp))
    for e in range(3):
        vt[e * 128:e * 128 + 128, :] = own_v[(e + 2) * 8:(e + 2) * 8 + 128].T.astype(BF)
    landed([zui, zue])
    sum_u = joined(sum_ue + zr_ue[...].astype(F32), sum_ui + zr_ui[...].astype(F32))[8:168]
    u = jax.nn.sigmoid(sum_u[:, :128] + biases[0:1, :])
    pre = sum_u[:, 128:] + biases[2:3, :] + cs[x].astype(F32)
    landed(cand)
    for d in range(3):
        pre = pre + cr[d].astype(F32)
    fresh = jnp.tanh(pre)
    h = hp[16:176, :]
    cot = cp[16:176, :]
    cg = (cot * u * (1.0 - fresh * fresh)).astype(BF)
    g1c[x] = cg
    got_c = [push(g1c.at[x], g1c.at[x], xpeer(d)) for d in (2, 1, 3)]
    ug = (cot * (fresh - h) * u * (1.0 - u)).astype(BF)
    g1u[x] = ug
    got_u = [push(g1u.at[x], g1u.at[x], xpeer(d)) for d in (2, 1, 3)]
    direct = (cot * (1.0 - u))[16:144]
    hn = ((1.0 - u) * h + u * fresh)[16:144]
    field_ref[:, :128] = own_a(hn).astype(BF)
    sum_c = jnp.sum(cg[16:144].astype(F32), axis=0, keepdims=True)
    sum_g = jnp.sum(ug[16:144].astype(F32), axis=0, keepdims=True)

    landed(got_c)
    grads = tiles(g1c)
    gg = shifted(dot_nt(grads, tiles(w_ch)), 0, 144)
    r_near = r[16:160]
    rt = (gg * hp[24:168, :] * r_near * (1.0 - r_near)).astype(BF).astype(F32)
    edge = jnp.zeros((8, 128), F32)
    g2[x] = jnp.concatenate([edge, rt, edge], axis=0).astype(BF)
    got_r = [push(g2.at[x], g2.at[x], xpeer(d)) for d in (2, 1, 3)]
    sum_q = jnp.sum(rt[8:136], axis=0, keepdims=True)
    bs[...] = jnp.where(row == 0, sum_g, jnp.where(row == 1, sum_q, jnp.where(row == 2, sum_c, 0.0)))
    bias1 = [push(bs, br.at[d - 1], mpeer(d)) for d in range(1, 8)]

    low = lax.broadcasted_iota(jnp.int32, (64, 128), 1) < 64

    def weight_grad(left_ref, grad_ref, place):
        left_rows = left_ref[...]
        for q in range(2):
            rhs = jnp.concatenate([grad_ref[2 * q, 16:144, :], grad_ref[2 * q + 1, 16:144, :]], axis=1)
            product = dot(left_rows, rhs)
            for e in range(3):
                t0 = product[e * 128:e * 128 + 128, :128]
                t1 = product[e * 128:e * 128 + 128, 128:]
                slabs = (
                    jnp.where(low, t0[64:], t0[:64]),
                    jnp.where(low, t1[64:], t1[:64]),
                    jnp.where(low, t0[:64] + roll(t0[64:], 64), t1[64:] + roll(t1[:64], 64)),
                )
                for k, slab in enumerate(slabs):
                    out_ref, n = place(e, q * 3 + k)
                    out_ref[n * 64:n * 64 + 64, :] = slab.astype(BF)

    def chunk(t, rows):
        return pl.ds(pl.multiple_of(t * rows, 16), rows)

    weight_grad(vt, g1c, lambda e, k: (blob_a, e * 6 + k))
    landed(got_u)
    weight_grad(ut, g1u, lambda e, k: (blob_a, 18 + e * 6 + k) if e < 2 else (blob_r, 18 + k))
    half = [push(blob_a.at[chunk(t * CN + 1 - core, 240), :], core_a.at[t], other_core) for t in range(4)]
    total = shifted(dot_nt(grads, tiles(w_cx)), 8, 128) + shifted(dot_nt(tiles(g1u), tiles(w_upd)), 8, 128)
    landed(got_r)
    weight_grad(ut, g2, lambda e, k: (blob_r, e * 6 + k))
    over_m = [push(blob_r.at[chunk((m + d) % 8, 192), :], m_r.at[d - 1], mpeer(d)) for d in range(1, 8)]
    landed(half)
    for t in range(4):
        mid_a[t] = (blob_a[chunk(t * CN + core, 240), :].astype(F32) + core_a[t].astype(F32)).astype(BF)
    over_y = [push(mid_a.at[(yy + d) % YN], y_a.at[d - 1], ypeer(d)) for d in (2, 1, 3)]
    total = total + shifted(dot_nt(tiles(g2), tiles(w_res)), 8, 128)
    hidden = own_b(direct + gg[8:136] * r[24:152])
    field_ref[:, 128:] = jnp.where(slot_a((128, 128)), total, hidden + total).astype(BF)

    def reduce_z(owners, mine, came, out, which):
        def copy(src, dst, send, recv, z):
            return pltpu.make_async_remote_copy(
                src_ref=src, dst_ref=dst, send_sem=send, recv_sem=recv, device_id=lpeer(z - zl), device_id_type=MESH
            )

        def up(i, s, p):
            return copy(mine.at[i], came.at[s], up_s.at[which, i], up_r.at[which, s], p)

        def down(i, d, z):
            return copy(out.at[i], out.at[i], down_s.at[which, d - 1], down_r.at[which, i], z)

        for i, p in enumerate(owners):
            pl.when(zl != p)(up(i, zl, p).start)

        def own():
            for i, p in enumerate(owners):
                @pl.when(zl == p)
                def _():
                    value = mine[i].astype(F32)
                    for s in range(8):
                        if s != p:
                            up(i, s, p).wait_recv()
                            value = value + came[s].astype(F32)
                    out[i] = value.astype(BF)
                    for d in range(1, 8):
                        down(i, d, (p + d) % 8).start()

        def back():
            for i, p in enumerate(owners):
                pl.when(zl != p)(down(i, 1, p).wait_recv)

        def close():
            for i, p in enumerate(owners):
                @pl.when(zl != p)
                def _():
                    up(i, zl, p).wait_send()

                @pl.when(zl == p)
                def _():
                    for d in range(1, 8):
                        down(i, d, (p + d) % 8).wait_send()

        return own, back, close

    acc = mid_a[yy].astype(F32)
    landed(over_y)
    for d in range(3):
        acc = acc + y_a[d].astype(F32)
    for p in range(3):
        zs_a[p] = acc[p * 80:p * 80 + 80].astype(BF)
    own_za, back_za, close_za = reduce_z((2, 3, 4), zs_a, zq_a, zf_a, 0)
    b1 = bs[...]
    landed(bias1)
    for d in range(7):
        b1 = b1 + br[d]
    bs2[...] = b1
    bias2 = [push(bs2, br2.at[d - 1], lpeer(d)) for d in range(1, 8)]
    acc = blob_r[chunk(m, 192), :].astype(F32)
    landed(over_m)
    for d in range(7):
        acc = acc + m_r[d].astype(F32)
    for p in range(2):
        zs_b[p] = acc[p * 96:p * 96 + 96].astype(BF)
    own_zb, back_zb, close_zb = reduce_z((3, 4), zs_b, zq_b, zf_b, 1)
    own_za()
    own_zb()

    def spread(fin):
        to_y = [push(fin.at[m], fin.at[m], ypeer(d)) for d in (2, 1, 3)]
        return to_y, [push(fin.at[m], fin.at[m], other_core)]

    def forward(fin, to_y, rest):
        for copy, d in zip(to_y, (2, 1, 3)):
            copy.wait_recv()
            at = ((yy + YN - d) % YN) * CN + core
            rest.append(push(fin.at[at], fin.at[at], other_core))

    back_za()
    for p in range(3):
        fin_a[m, p * 80:p * 80 + 80, :] = zf_a[p]
    to_ya, rest_a = spread(fin_a)
    back_zb()
    for p in range(2):
        fin_r[m, p * 96:p * 96 + 96, :] = zf_b[p]
    to_yr, rest_r = spread(fin_r)
    b2 = bs2[...]
    landed(bias2)
    for d in range(7):
        b2 = b2 + br2[d]
    bias_ref[...] = own_a(b2)
    forward(fin_r, to_yr, rest_r)
    forward(fin_a, to_ya, rest_a)
    landed(rest_a)
    landed(rest_r)
    close_za()
    close_zb()
    for copy in sends:
        copy.wait_send()


def finish(
    reset_ref, field_ref, fin_a, fin_r, bias_ref, q5_ref, pm_ref,
    hn_ref, gx_ref, gh_ref, wgg_out, gb_ref, wgc_out, cb_ref,
    wgg_ref, wgc_ref, sems,
):
    def slab_a(n):
        pieces = [fin_a[r // 240, r % 240:r % 240 + 16, :] for r in range(n * 64, n * 64 + 64, 16)]
        return jnp.concatenate(pieces, axis=0)

    def slab_r(n):
        return fin_r[n // 3, n % 3 * 64:n % 3 * 64 + 64, :]

    def put(gate, a, e, value):
        for s in range(2):
            part = value[s * 32:s * 32 + 32]
            if gate is None:
                wgc_ref[s, a, e] = part
            else:
                later[s].append((a, e, gate, part))

    later = ([], [])
    q5 = q5_ref[...]
    for gate in (None, 0, 1):
        def get(e, q, k):
            n = e * 6 + q * 3 + k
            if gate is None:
                return slab_a(n)
            if gate == 1:
                return slab_r(n)
            return slab_a(18 + n) if e < 2 else slab_r(6 + n)

        outer = jnp.concatenate(
            [
                jnp.concatenate([get(e, q, k) for q in range(2) for k in range(2)], axis=1)
                for e in range(3)
            ],
            axis=0,
        )
        outer = dot(outer, q5)
        for e in range(3):
            at = slice(e * 64, e * 64 + 64)
            put(gate, 2, e, outer[at, :256])
            put(gate, 0, e, outer[at, 256:])
            inner = jnp.concatenate([get(e, q, 2) for q in range(2)], axis=1)
            put(gate, 1, e, inner.astype(F32))
        if gate is None:
            copies = [pltpu.make_async_copy(wgc_ref, wgc_out, sems.at[0])]
            copies[0].start()
    for s in range(2):
        for a, e, gate, part in later[s]:
            wgg_ref[s, a, e, :, gate, :] = part
        copies.append(pltpu.make_async_copy(wgg_ref.at[s], wgg_out.at[s], sems.at[1 + s]))
        copies[-1].start()

    rows = dot(pm_ref[...], field_ref[...])
    for i in range(2):
        hn_ref[:, i] = rows[:, i * 64:i * 64 + 32].reshape(8, 16, 32).astype(BF)
        gx_ref[:, i] = rows[:, 128 + i * 64:160 + i * 64].reshape(8, 16, 32).astype(BF)
        value = rows[:, 160 + i * 64:192 + i * 64].reshape(8, 16, 32)
        for b in range(8):
            gh_ref[b, i] = (value[b] * (1 - reset_ref[b]).astype(F32)).astype(BF)
    sums = bias_ref[...]
    sums = sums + roll(sums, 64)
    gb_ref[...] = sums[0:2, 0:32]
    cb_ref[...] = sums[2:3, 0:32]
    for copy in copies:
        copy.wait()


def per_device(x_in, h_prev, reset, w_gate, gate_bias, w_cand, cand_bias, cotangent):
    def bf(*shape):
        return pltpu.VMEM(shape, BF)

    def f32(*shape):
        return pltpu.VMEM(shape, F32)

    scratch = [
        bf(128, 256), bf(32, 256), bf(32, 256), f32(192, 128), bf(32, 128), bf(32, 128), bf(128, 128),
        f32(192, 128), f32(192, 128), bf(8, 48, 256), bf(2, 288, 256),
        bf(4, 384, 128), bf(4, 384, 128), bf(4, 384, 128), bf(4, 384, 128),
        f32(8, 128), f32(8, 128), bf(4, 112, 128), bf(3, 112, 128), bf(4, 112, 256), bf(3, 112, 256),
        bf(4, 64, 128), bf(3, 64, 128), bf(4, 64, 256), bf(3, 64, 256),
        bf(112, 128), bf(112, 128), bf(112, 256), bf(112, 256), bf(64, 128), bf(64, 128), bf(64, 256), bf(64, 256),
        f32(176, 128), bf(4, 160, 128), bf(3, 160, 128),
        bf(4, 160, 128), bf(4, 160, 128), bf(4, 160, 128), bf(384, 128), bf(384, 128),
        bf(1920, 128), bf(1536, 128), bf(4, 240, 128), bf(4, 240, 128), bf(3, 240, 128), bf(7, 192, 128),
        bf(3, 80, 128), bf(8, 80, 128), bf(3, 80, 128), bf(2, 96, 128), bf(8, 96, 128), bf(2, 96, 128),
        f32(8, 128), f32(7, 8, 128), f32(8, 128), f32(7, 8, 128),
        pltpu.SemaphoreType.DMA((COPIES,)), pltpu.SemaphoreType.DMA((COPIES,)),
        pltpu.SemaphoreType.DMA((2, 4)), pltpu.SemaphoreType.DMA((2, 8)),
        pltpu.SemaphoreType.DMA((2, 7)), pltpu.SemaphoreType.DMA((2, 4)),
    ]
    q5 = jnp.asarray(block_transpose(4, 2, 64), BF)
    rows_in = jnp.asarray(row_order(), BF)
    rows_out = jnp.asarray(row_order().T, BF)
    near = lambda v: v.transpose(1, 2, 3, 0)
    smem = pl.BlockSpec(memory_space=pltpu.SMEM)
    whole = pl.BlockSpec(memory_space=pltpu.VMEM)
    field, fin_a, fin_r, bias = pl.pallas_call(
        kernel,
        out_shape=(
            jax.ShapeDtypeStruct((128, 256), BF),
            jax.ShapeDtypeStruct((8, 240, 128), BF),
            jax.ShapeDtypeStruct((8, 192, 128), BF),
            jax.ShapeDtypeStruct((8, 128), F32),
        ),
        in_specs=[smem] + [whole] * 9,
        out_specs=[whole] * 4,
        scratch_shapes=scratch,
        compiler_params=pltpu.CompilerParams(
            collective_id=0, has_side_effects=True, vmem_limit_bytes=48 * 1024 * 1024
        ),
        cost_estimate=pl.CostEstimate(flops=1_000_000_000, bytes_accessed=8_000_000, transcendentals=100_000),
    )(
        reset, near(x_in), near(h_prev), near(cotangent), w_gate.reshape(576, 512), w_cand.reshape(576, 256),
        gate_bias, cand_bias.reshape(1, 32), q5, rows_in,
    )
    shape = jax.ShapeDtypeStruct((8, 2, 16, 32), BF)
    h_new, grad_x, grad_h, wgg, gb, wgc, cb = pl.pallas_call(
        finish,
        out_shape=(
            shape, shape, shape,
            jax.ShapeDtypeStruct(w_gate.shape, F32), jax.ShapeDtypeStruct((2, 32), F32),
            jax.ShapeDtypeStruct(w_cand.shape, F32), jax.ShapeDtypeStruct((1, 32), F32),
        ),
        in_specs=[smem] + [whole] * 6,
        out_specs=[whole, whole, whole, pl.BlockSpec(memory_space=pl.ANY), whole, pl.BlockSpec(memory_space=pl.ANY), whole],
        scratch_shapes=[f32(*w_gate.shape), f32(*w_cand.shape), pltpu.SemaphoreType.DMA((3,))],
        compiler_params=pltpu.CompilerParams(vmem_limit_bytes=32 * 1024 * 1024),
    )(reset, field, fin_a, fin_r, bias, q5, rows_out)
    back = lambda v: v.transpose(3, 0, 1, 2)
    return back(h_new), back(grad_x), back(grad_h), wgg, gb, wgc, cb.reshape(32)


def solution(mesh):
    field = P("filt", None, None, "wedge")
    in_specs = (
        field, field, P(), P(None, None, None, "filt", None, None), P(None, "filt"),
        P(None, None, None, "filt", None), P("filt"), field,
    )
    out_specs = (
        field, field, field, P(None, None, None, "filt", None, None), P(None, "filt"),
        P(None, None, None, "filt", None), P("filt"),
    )
    return jax.shard_map(per_device, mesh=mesh, in_specs=in_specs, out_specs=out_specs, check_vma=False)
```
